256 devices in a mesh: wide: 64 (over y, z, core), narrow: 4 (over x).
Axes of the slice: x: 4, y: 4, z: 8, core: 2. Of those that a mesh axis runs over, the one named last changes fastest.
Arguments:
- tensor_blocks: bfloat16 [6144, 64, 4096], P(('wide', 'narrow')), may hold values from -6 to 6
- block_rows: int32 [6144], P(('wide', 'narrow')), may hold values from 0 to 255, as said below
- block_seconds: int32 [6144], P(('wide', 'narrow')), may hold values from 0 to 511, as said below
- block_thirds: int32 [6144], P(('wide', 'narrow')), may hold values from 0 to 127, as said below
- second_factor: bfloat16 [32768, 256], P('wide')
- third_factor: bfloat16 [8192, 256], P('wide')
Outputs:
- new_factor: float32 [16384, 256], P(('wide', 'narrow'))
The draws below stay inside these ranges and needn't reach their ends.
Inputs may be any that keep to these rules, and one draw needn't show every extreme that they name: `block_rows`: blocks d * 24 to (d + 1) * 24 - 1 lie on device d of wide+narrow; their mode-1 row blocks lie in w * 4 to (w + 1) * 4 - 1, w being the device's index along wide. `block_seconds`: row block j of second_factor is held by index j // 8 of wide. Among the blocks of all devices of one index of wide together, at most 4 name row blocks held by one index of wide; in every draw one index of wide, the same for all, is named by exactly 4 blocks of every index of wide. `block_thirds`: row block k of third_factor is held by index k // 2 of wide. Among the blocks of all devices of one index of wide together, at most 4 name row blocks held by one index of wide; in every draw one index of wide, the same for all, is named by exactly 4 blocks of every index of wide.
All inputs are finite; a program needn't handle non-finite values.
Results may differ from the reference program's by a relative error of at most 0.0034.
Values may be sent and summed in bfloat16 or wider, within the bound.
No kernel may reach another device: no remote copies, remote signals or barrier semaphores. Data moves between devices by JAX's collectives and lax.ppermute only.
A program may use at most 128 MiB of HBM per device.

```python
import math
import jax
import jax.numpy as jnp
from jax import lax

BS = 64
R = 256
BLK_DEV = 24
R1_DEV = 4
R2_DEV = 8
R3_DEV = 2
BLOCKS = 6144
BLK_ONE = 256
BLK_TWO = 512
BLK_THREE = 128
ROWS_ONE = 16384
ROWS_TWO = 32768
ROWS_THREE = 8192
CAP = 4


def column_logs(key):
    return jax.random.uniform(jax.random.fold_in(key, 5), (R,), jnp.float32, 0.0, math.log(10.0))


def factor_rows(key, jitter, common_weight, spread, factor_scale, columns):
    number = jitter.shape[0]
    scale_key, common_key = jax.random.split(key)
    rising = jnp.exp(0.5 * math.log(3.0) * jnp.arange(number, dtype=jnp.float32) / number)
    row_scale = jnp.exp(jax.random.uniform(scale_key, (number,), jnp.float32, 0.0, spread)) * rising
    shared = jax.random.normal(common_key, (number, 1), jnp.float32)
    return factor_scale / math.sqrt(39.0) * row_scale[:, None] * (jitter + common_weight * shared) * columns[None, :]


def draw_second_factor(key, part):
    columns = jnp.exp(column_logs(key))
    key = jax.random.fold_in(key, 21)
    noise_key, rest_key = jax.random.split(key)
    jitter = jax.random.normal(noise_key, (ROWS_TWO, R), jnp.float32)
    common_weight = 0.6
    spread = math.log(10.0)
    factor_scale = BS / ROWS_TWO
    return factor_rows(rest_key, jitter, common_weight, spread, factor_scale, columns).astype(jnp.bfloat16)


def draw_third_factor(key, part):
    columns = jnp.exp(-column_logs(key))
    key = jax.random.fold_in(key, 23)
    noise_key, rest_key = jax.random.split(key)
    jitter = jax.random.normal(noise_key, (ROWS_THREE, R), jnp.float32)
    common_weight = 0.6
    spread = math.log(10.0)
    factor_scale = math.sqrt(BLOCKS / BLK_ONE) / ROWS_THREE
    return factor_rows(rest_key, jitter, common_weight, spread, factor_scale, columns).astype(jnp.bfloat16)


def capped_blocks(key, per_holder):
    holders = BLK_ONE // R1_DEV
    devices = BLOCKS // BLK_DEV
    narrow_count = devices // holders
    pooled = BLK_DEV * narrow_count
    total_places = holders * CAP
    hot_key, group_key = jax.random.split(key)
    hottest = jax.random.randint(hot_key, (), 0, holders)

    def one_group(group_seed):
        order_key, within_key, shuffle_key = jax.random.split(group_seed, 3)
        serial = jax.random.permutation(order_key, total_places)
        holder = serial // CAP
        ranking = jnp.where(holder == hottest, serial % CAP - CAP, jnp.arange(total_places))
        chosen = serial[jnp.argsort(ranking, stable=True)][:pooled] // CAP
        within = jax.random.randint(within_key, (pooled,), 0, per_holder)
        picked = chosen * per_holder + within
        return picked[jax.random.permutation(shuffle_key, pooled)]
    return jax.vmap(one_group)(jax.random.split(group_key, holders)).reshape(-1).astype(jnp.int32)


def draw_block_rows(key, part):
    key = jax.random.fold_in(key, 31)
    devices = BLOCKS // BLK_DEV
    narrow_count = devices // (BLK_ONE // R1_DEV)
    wide_index = jnp.arange(BLOCKS) // BLK_DEV // narrow_count
    return (wide_index * R1_DEV + jax.random.randint(key, (BLOCKS,), 0, R1_DEV)).astype(jnp.int32)


def draw_block_seconds(key, part):
    key = jax.random.fold_in(key, 41)
    return capped_blocks(key, R2_DEV)


def draw_block_thirds(key, part):
    key = jax.random.fold_in(key, 43)
    return capped_blocks(key, R3_DEV)


def level_of(stream_key, shape, cuts, smallest, top_value):
    def one(position, parts):
        steps = jax.random.uniform(jax.random.fold_in(jax.random.fold_in(stream_key, 6), position), (parts,), jnp.float32, smallest / len(cuts), top_value / len(cuts))
        return jnp.repeat(jnp.exp(steps), shape[position] // parts).reshape((-1,) + (1,) * (len(shape) - position - 1))

    level = one(*cuts[0])
    for cut in cuts[1:]:
        level = level * one(*cut)
    return level


def centred(own_key, extent, deviation, bound, cuts=(), kind=jnp.bfloat16):
    drawn = jax.random.normal(own_key, extent, jnp.float32) * deviation
    if len(cuts) > 0:
        drawn = level_of(own_key, extent, cuts, -0.22, 0.18) * drawn
    return jnp.clip(drawn, min=-bound, max=bound).astype(kind)


def setup_inputs(seed: int = 0) -> dict:
    streams_of = jax.random.split(jax.random.key(seed), 7)
    tensor_blocks = centred(streams_of[0], (BLOCKS, BS, BS * BS), 1.0, 6.0, ((0, 256),))
    block_rows = draw_block_rows(jax.random.fold_in(streams_of[6], 71), 0)
    block_seconds = draw_block_seconds(jax.random.fold_in(streams_of[6], 71), 0)
    block_thirds = draw_block_thirds(jax.random.fold_in(streams_of[6], 71), 0)
    second_factor = draw_second_factor(jax.random.fold_in(streams_of[6], 71), 0)
    third_factor = draw_third_factor(jax.random.fold_in(streams_of[6], 71), 0)
    return {"tensor_blocks": tensor_blocks, "block_rows": block_rows, "block_seconds": block_seconds, "block_thirds": block_thirds, "second_factor": second_factor, "third_factor": third_factor}


def reference(tensor_blocks, block_rows, block_seconds, block_thirds, second_factor, third_factor):
    group_size = math.gcd(BLOCKS, 16)
    seconds = second_factor.reshape(BLK_TWO, BS, R)
    thirds = third_factor.reshape(BLK_THREE, BS, R)

    def accumulate(summed, inputs):
        blocks, rows_one, rows_two, rows_three = inputs
        left_rows = jnp.take(seconds, rows_two, axis=0).astype(jnp.float32)
        right_rows = jnp.take(thirds, rows_three, axis=0).astype(jnp.float32)
        product = (left_rows[:, :, None, :] * right_rows[:, None, :, :]).reshape(group_size, BS * BS, R)
        product = lax.optimization_barrier(product.astype(jnp.bfloat16)).astype(jnp.float32)
        pieces = jnp.einsum('tak,tkr->tar', blocks.astype(jnp.float32), product, precision=lax.Precision.HIGHEST)
        return (summed + jax.ops.segment_sum(pieces, rows_one, num_segments=BLK_ONE), None)
    stacked = (tensor_blocks.reshape(-1, group_size, BS, BS * BS), block_rows.reshape(-1, group_size), block_seconds.reshape(-1, group_size), block_thirds.reshape(-1, group_size))
    summed, unused = lax.scan(accumulate, jnp.zeros((BLK_ONE, BS, R), jnp.float32), stacked)
    mttkrp = summed.reshape(ROWS_ONE, R)
    gram_second = jnp.dot(second_factor.T.astype(jnp.float32), second_factor.astype(jnp.float32), preferred_element_type=jnp.float32)
    gram_third = jnp.dot(third_factor.T.astype(jnp.float32), third_factor.astype(jnp.float32), preferred_element_type=jnp.float32)
    normal = gram_second * gram_third
    cholesky_factor = jnp.linalg.cholesky(normal)
    halfway = lax.linalg.triangular_solve(cholesky_factor, mttkrp, left_side=False, lower=True, transpose_a=True)
    return lax.linalg.triangular_solve(cholesky_factor, halfway, left_side=False, lower=True)
```

```python
import functools
import jax
import jax.numpy as jnp
from jax import lax
from jax.experimental import pallas as pl
from jax.experimental.pallas import tpu as pltpu
from jax.sharding import Mesh, PartitionSpec as P

BS = 64
R = 256
BLK = 24
YS, ZS, CS, XS = 4, 8, 2, 4
PEERS = YS * CS * XS
RING = ("y", "c", "x")
ROWS0 = 32
ROWS1 = 192
ROWS2 = 112
F32 = jnp.float32
BF16 = jnp.bfloat16
VMEM = pl.BlockSpec(memory_space=pltpu.VMEM)
SMEM = pl.BlockSpec(memory_space=pltpu.SMEM)
LIMIT = 48 * 1024 * 1024


def call(kernel, out_shape, in_specs, scratch=(), **kw):
    return pl.pallas_call(
        kernel,
        out_shape=out_shape,
        in_specs=in_specs,
        out_specs=jax.tree.map(lambda _: VMEM, out_shape),
        scratch_shapes=list(scratch),
        compiler_params=pltpu.CompilerParams(vmem_limit_bytes=LIMIT),
        **kw,
    )


def three(value):
    high = value.astype(BF16).astype(F32)
    rest = value - high
    middle = rest.astype(BF16).astype(F32)
    return high, middle, rest - middle


def halves(rows):
    return pltpu.VMEM((2, rows, 128), F32)


def put(wide, start, stride, values):
    for half in range(2):
        wide[half, pl.ds(start, PEERS, stride=stride), :] = values[:, 128 * half : 128 * half + 128]


def take(wide, start, stride):
    return jnp.concatenate([wide[half, pl.ds(start, PEERS, stride=stride), :] for half in range(2)], axis=1)


def fill(wide, values):
    for half in range(2):
        wide[half] = values[:, 128 * half : 128 * half + 128]


def whole(wide):
    return jnp.concatenate([wide[half] for half in range(2)], axis=1)


def packed_gram(rows):
    gram = lax.dot_general(rows, rows, (((0,), (0,)), ((), ())), preferred_element_type=F32)
    half = R // 2
    down = lax.broadcasted_iota(jnp.int32, (half, half), 0)
    along = lax.broadcasted_iota(jnp.int32, (half, half), 1)
    corner = gram[half:, half:]
    mixed = jnp.where(down >= along, gram[:half, :half], corner)
    diagonal = jnp.sum(jnp.where(down == along, corner, 0.0), axis=1, keepdims=True)
    return jnp.concatenate([mixed, gram[half:, :half]], axis=1), diagonal


def first_kernel(x_ref, second_ref, third_ref, seconds_ref, thirds_ref, out_ref, wide, spot):
    x = x_ref[0]
    rows_two = second_ref[pl.ds(pl.multiple_of(x * 128, 128), 128), :]
    rows_three = third_ref[pl.ds(pl.multiple_of(x * 32, 32), 32), :]
    lane = lax.broadcasted_iota(jnp.int32, (PEERS, R), 1)
    extra = [jnp.zeros((PEERS, R), F32) for _ in range(3)]
    for which, rows in enumerate((rows_two, rows_three)):
        packed, diagonal = packed_gram(rows)
        for part, values in enumerate(three(packed)):
            for m in range(4):
                put(wide, 12 * which + 4 * part + m, ROWS0, values[32 * m : 32 * m + 32, :])
        for part, values in enumerate(three(diagonal)):
            for m in range(4):
                extra[part] = jnp.where(
                    lane == 128 + 4 * which + m, values[32 * m : 32 * m + 32, :], extra[part]
                )
    pieces = rows_two.astype(F32)
    for n in range(4):
        put(wide, 24 + n, ROWS0, pieces[32 * n : 32 * n + 32, :])
    put(wide, 28, ROWS0, rows_three.astype(F32))
    seconds = seconds_ref[...]
    names = (seconds >> 4, seconds & 15, thirds_ref[...])
    for part in range(3):
        spot[...] = extra[part]
        spot[:, 0:BLK] = jnp.broadcast_to(names[part].astype(F32), (PEERS, BLK))
        put(wide, 29 + part, ROWS0, spot[...])
    out_ref[...] = whole(wide).astype(BF16).reshape(PEERS, ROWS0, R)


def second_kernel(got_ref, out_ref, wide, slab):
    fill(wide, got_ref[...].reshape(PEERS * ROWS0, R).astype(F32))
    total = got_ref[0].astype(F32)
    for source in range(1, PEERS):
        total = total + got_ref[source].astype(F32)
    for i in range(2):
        for u in range(2):
            slab[64 * i + 32 * u : 64 * i + 32 * u + 32, :] = take(wide, 24 + 2 * u + i, ROWS0)
    slab[128:160, :] = take(wide, 28, ROWS0)
    chunks = [total[12 * w : 12 * w + 4] + total[12 * w + 4 : 12 * w + 8] + total[12 * w + 8 : 12 * w + 12] for w in range(2)]
    for w in range(2):
        for part, values in enumerate(three(chunks[w])):
            slab[160 + 12 * w + 4 * part : 164 + 12 * w + 4 * part, :] = values
    slab[184:192, :] = jnp.zeros((8, R), F32)
    for part, values in enumerate(three(total[29:30] + total[30:31] + total[31:32])):
        slab[184 + part : 185 + part, :] = values
    narrow = slab[...].astype(BF16)
    for z in range(ZS):
        out_ref[z] = narrow


def third_kernel(got_ref, pick_two_ref, pick_left_ref, pick_right_ref, out_ref, wide):
    for i in range(2):
        table = got_ref[:, 64 * i : 64 * i + 64, :].reshape(64 * ZS, R)
        rows = jnp.dot(pick_two_ref[...], table, preferred_element_type=F32)
        for d in range(PEERS):
            wide[d * ROWS2 + BLK * i : d * ROWS2 + BLK * (i + 1), :] = rows[BLK * d : BLK * (d + 1)]
    table = got_ref[:, 128:160, :].reshape(32 * ZS, R)
    for i, pick_ref in enumerate((pick_left_ref, pick_right_ref)):
        rows = jnp.dot(pick_ref[...], table, preferred_element_type=F32)
        for d in range(PEERS):
            wide[d * ROWS2 + BLK * (2 + i) : d * ROWS2 + BLK * (3 + i), :] = rows[BLK * d : BLK * (d + 1)]
    total = got_ref[0, 160:192, :].astype(F32)
    for z in range(1, ZS):
        total = total + got_ref[z, 160:192, :].astype(F32)
    gram_two = total[0:4] + total[4:8] + total[8:12]
    gram_three = total[12:16] + total[16:20] + total[20:24]
    normal = three(gram_two * gram_three)
    diagonal = total[24:25] + total[25:26] + total[26:27]
    diagonal = three(diagonal[:, 128:132] * diagonal[:, 132:136])
    for part in range(3):
        wide[96 + 4 * part : 100 + 4 * part, :] = normal[part]
    wide[108:112, :] = jnp.zeros((4, R), F32)
    for part in range(3):
        wide[108 + part : 109 + part, 128:132] = diagonal[part]
    tail = wide[96:112, :]
    for d in range(1, PEERS):
        wide[d * ROWS2 + 96 : d * ROWS2 + 112, :] = tail
    out_ref[...] = wide[...].astype(BF16).reshape(PEERS, ROWS2, R)


def product_kernel(target_ref, block_ref, got_ref, out_ref, wide):
    t = pl.program_id(0)

    @pl.when(t == 0)
    def _():
        fill(wide, got_ref[...].reshape(PEERS * ROWS2, R).astype(F32))
        out_ref[...] = jnp.zeros_like(out_ref)

    left = [take(wide, BLK * i + t, ROWS2) for i in range(2)]
    right = jnp.concatenate([take(wide, BLK * (2 + i) + t, ROWS2) for i in range(2)], axis=0)
    right = right.astype(BF16)
    total = jnp.zeros((BS, R), F32)
    for q in range(BS // 4):
        parts = []
        for b in range(4 * q, 4 * q + 4):
            row = left[b // 32][b % 32 : b % 32 + 1, :]
            row = jnp.broadcast_to(row, (16, R)).astype(BF16)
            parts.append(jnp.concatenate([row] * 4, axis=0) * right)
        total = total + jnp.dot(
            block_ref[0, :, 256 * q : 256 * q + 256],
            jnp.concatenate(parts, axis=0),
            preferred_element_type=F32,
        )
    place = pl.multiple_of(target_ref[t] * BS, BS)
    out_ref[pl.ds(place, BS), :] += total


def products(targets, tensor_blocks, got):
    return pl.pallas_call(
        product_kernel,
        out_shape=jax.ShapeDtypeStruct((XS * BS, R), F32),
        grid_spec=pltpu.PrefetchScalarGridSpec(
            num_scalar_prefetch=1,
            grid=(BLK,),
            in_specs=[
                pl.BlockSpec((1, BS, BS * BS), lambda t, _: (t, 0, 0)),
                pl.BlockSpec((PEERS, ROWS2, R), lambda t, _: (0, 0, 0)),
            ],
            out_specs=pl.BlockSpec((XS * BS, R), lambda t, _: (0, 0)),
            scratch_shapes=[halves(PEERS * ROWS2)],
        ),
        compiler_params=pltpu.CompilerParams(
            vmem_limit_bytes=LIMIT, dimension_semantics=("arbitrary",)
        ),
        cost_estimate=pl.CostEstimate(
            flops=2 * BLK * BS * BS * BS * R, bytes_accessed=BLK * BS * BS * BS * 2, transcendentals=0
        ),
    )(targets, tensor_blocks, got)


def dot_high(a, b, dims=((1,), (0,))):
    return lax.dot_general(
        a, b, (dims, ((), ())), precision=lax.Precision.HIGHEST, preferred_element_type=F32
    )


def inverse_of_lower(matrix, down, along):
    size = R // 2
    joined = jnp.concatenate([matrix, jnp.where(down == along, 1.0, 0.0).astype(F32)], axis=1)
    groups = [joined[8 * g : 8 * g + 8] for g in range(size // 8)]
    sub = lax.broadcasted_iota(jnp.int32, (8, 1), 0)
    for k in range(size):
        g0, r0 = divmod(k, 8)
        pivot_row = groups[g0][r0 : r0 + 1, :]
        scaled = pivot_row * (1.0 / pivot_row[:, k : k + 1])
        for g in range(g0, size // 8):
            column = groups[g][:, k : k + 1]
            if g == g0:
                column = jnp.where(sub > r0, column, 0.0)
            groups[g] = groups[g] - column * scaled
    joined = jnp.concatenate(groups, axis=0)
    pivots = jnp.sum(jnp.where(down == along, joined[:, :size], 0.0), axis=1, keepdims=True)
    root = lax.rsqrt(pivots)
    root = root * (1.5 - 0.5 * pivots * root * root)
    return joined[:, size:] * root


def cholesky_kernel(got_ref, out_ref, wide):
    half = R // 2
    fill(wide, got_ref[...].reshape(PEERS * 16, R).astype(F32))
    packed, diagonal = [], []
    for m in range(4):
        rows = [take(wide, 4 * part + m, 16) for part in range(3)]
        packed.append(rows[0] + rows[1] + rows[2])
        rows = [take(wide, 12 + part, 16) for part in range(3)]
        diagonal.append((rows[0] + rows[1] + rows[2])[:, 128 + m : 129 + m])
    packed = jnp.concatenate(packed, axis=0)
    diagonal = jnp.concatenate(diagonal, axis=0)
    down = lax.broadcasted_iota(jnp.int32, (half, half), 0)
    along = lax.broadcasted_iota(jnp.int32, (half, half), 1)
    mixed = packed[:, :half]
    flipped = mixed.T
    upper = jnp.where(down >= along, mixed, flipped)
    corner = jnp.where(down == along, diagonal, jnp.where(down < along, mixed, flipped))
    below = packed[:, half:]
    first = inverse_of_lower(upper, down, along)
    lower = dot_high(below, first, ((1,), (1,)))
    rest = corner - dot_high(lower, lower, ((1,), (1,)))
    middle = dot_high(lower, first)
    last = inverse_of_lower(rest, down, along)
    out_ref[:half, :half] = first
    out_ref[:half, half:] = jnp.zeros((half, half), F32)
    out_ref[half:, :half] = -dot_high(last, middle)
    out_ref[half:, half:] = last


def cholesky_inverse(got):
    return pl.pallas_call(
        cholesky_kernel,
        out_shape=jax.ShapeDtypeStruct((R, R), F32),
        grid=(1,),
        in_specs=[pl.BlockSpec((PEERS, 16, R), lambda i: (0, 6, 0))],
        out_specs=pl.BlockSpec((R, R), lambda i: (0, 0)),
        scratch_shapes=[halves(PEERS * 16)],
        compiler_params=pltpu.CompilerParams(vmem_limit_bytes=LIMIT),
        cost_estimate=pl.CostEstimate(flops=10**9, bytes_accessed=10**6, transcendentals=0),
    )(got)


def final_kernel(parts_ref, inverse_ref, out_ref):
    rows = (parts_ref[0] + parts_ref[1]) + (parts_ref[2] + parts_ref[3])
    inverse = inverse_ref[...]
    halfway = dot_high(rows, inverse, ((1,), (1,)))
    out_ref[...] = dot_high(halfway, inverse)


def body(tensor_blocks, block_rows, block_seconds, block_thirds, second_factor, third_factor):
    shape = jax.ShapeDtypeStruct
    exchange = functools.partial(lax.all_to_all, split_axis=0, concat_axis=0, tiled=True)
    x = lax.axis_index("x").astype(jnp.int32).reshape(1)
    wide_at = (lax.axis_index("y") * ZS + lax.axis_index("z")) * CS + lax.axis_index("c")
    targets = block_rows - wide_at * XS

    sent = call(
        first_kernel,
        shape((PEERS, ROWS0, R), BF16),
        [SMEM, VMEM, VMEM, VMEM, VMEM],
        [halves(PEERS * ROWS0), pltpu.VMEM((PEERS, R), F32)],
    )(x, second_factor, third_factor, block_seconds.reshape(1, BLK), block_thirds.reshape(1, BLK))
    got0 = exchange(sent, RING)

    sent = call(
        second_kernel,
        shape((ZS, ROWS1, R), BF16),
        [VMEM],
        [halves(PEERS * ROWS0), pltpu.VMEM((ROWS1, R), F32)],
    )(got0)
    got1 = exchange(sent, "z")

    names = got0[:, 29:32, :BLK].astype(jnp.int32)
    seconds = (names[:, 0] * 16 + names[:, 1]).reshape(-1)
    thirds = names[:, 2].reshape(-1)

    def source(holder):
        return (holder // (ZS * CS)) * CS + holder % CS, holder // CS % ZS

    pair, plane = source(seconds // 8)
    place_two = plane * 64 + seconds % 2 * 32 + pair * XS + seconds % 8 // 2
    pair, plane = source(thirds // 2)
    place_three = plane * 32 + pair * XS + thirds % 2 * 2

    def one_hot(place, width):
        return (place[:, None] == jnp.arange(width)[None, :]).astype(BF16)

    sent = call(
        third_kernel,
        shape((PEERS, ROWS2, R), BF16),
        [VMEM] * 4,
        [pltpu.VMEM((PEERS * ROWS2, R), F32)],
    )(got1, one_hot(place_two, 64 * ZS), one_hot(place_three, 32 * ZS), one_hot(place_three + 1, 32 * ZS))
    got2 = exchange(sent, RING)

    summed = products(targets, tensor_blocks, got2)
    parts = exchange(summed.reshape(XS, BS, R), "x")
    inverse = cholesky_inverse(got2)
    return call(final_kernel, shape((BS, R), F32), [VMEM] * 2)(parts, inverse)


def solution(mesh):
    fine = Mesh(mesh.devices.reshape(YS, ZS, CS, XS), ("y", "z", "c", "x"))
    wide, every = ("y", "z", "c"), ("y", "z", "c", "x")
    in_specs = (
        P(every, None, None),
        P(every),
        P(every),
        P(every),
        P(wide, None),
        P(wide, None),
    )
    return jax.shard_map(body, mesh=fine, in_specs=in_specs, out_specs=P(every, None), check_vma=False)
```

```python
import functools
import jax
import jax.numpy as jnp
from jax import lax
from jax.experimental import pallas as pl
from jax.experimental.pallas import tpu as pltpu
from jax.sharding import Mesh, PartitionSpec as P

BS = 64
R = 256
BLK = 24
YS, ZS, CS, XS = 4, 8, 2, 4
PEERS = YS * CS * XS
RING = ("y", "c", "x")
ROWS0 = 32
ROWS1 = 192
ROWS2 = 112
F32 = jnp.float32
BF16 = jnp.bfloat16
VMEM = pl.BlockSpec(memory_space=pltpu.VMEM)
SMEM = pl.BlockSpec(memory_space=pltpu.SMEM)
HBM = pl.BlockSpec(memory_space=pltpu.HBM)
LIMIT = 48 * 1024 * 1024


def call(kernel, out_shape, in_specs, scratch=(), **kw):
    return pl.pallas_call(
        kernel,
        out_shape=out_shape,
        in_specs=in_specs,
        out_specs=jax.tree.map(lambda _: VMEM, out_shape),
        scratch_shapes=list(scratch),
        compiler_params=pltpu.CompilerParams(vmem_limit_bytes=LIMIT),
        **kw,
    )


def three(value):
    high = value.astype(BF16).astype(F32)
    rest = value - high
    middle = rest.astype(BF16).astype(F32)
    return high, middle, rest - middle


def halves(rows):
    return pltpu.VMEM((2, rows, 128), F32)


def put(wide, start, stride, values):
    for half in range(2):
        wide[half, pl.ds(start, PEERS, stride=stride), :] = values[:, 128 * half : 128 * half + 128]


def take(wide, start, stride):
    return jnp.concatenate([wide[half, pl.ds(start, PEERS, stride=stride), :] for half in range(2)], axis=1)


def fill(wide, values):
    for half in range(2):
        wide[half] = values[:, 128 * half : 128 * half + 128]


def whole(wide):
    return jnp.concatenate([wide[half] for half in range(2)], axis=1)


def packed_gram(rows):
    gram = lax.dot_general(rows, rows, (((0,), (0,)), ((), ())), preferred_element_type=F32)
    half = R // 2
    down = lax.broadcasted_iota(jnp.int32, (half, half), 0)
    along = lax.broadcasted_iota(jnp.int32, (half, half), 1)
    corner = gram[half:, half:]
    mixed = jnp.where(down >= along, gram[:half, :half], corner)
    diagonal = jnp.sum(jnp.where(down == along, corner, 0.0), axis=1, keepdims=True)
    return jnp.concatenate([mixed, gram[half:, :half]], axis=1), diagonal


def first_kernel(x_ref, second_ref, third_ref, seconds_ref, thirds_ref, out_ref, wide, spot, two, few, at, sems):
    x = x_ref[0]
    copies = [
        pltpu.make_async_copy(second_ref.at[pl.ds(pl.multiple_of(x * 128, 128), 128), :], two, sems.at[0]),
        pltpu.make_async_copy(third_ref.at[pl.ds(pl.multiple_of(x * 32, 32), 32), :], few, sems.at[1]),
        pltpu.make_async_copy(seconds_ref, at.at[0], sems.at[2]),
        pltpu.make_async_copy(thirds_ref, at.at[1], sems.at[3]),
    ]
    for copy in copies:
        copy.start()
    for copy in copies:
        copy.wait()
    rows_two = two[...]
    rows_three = few[...]
    lane = lax.broadcasted_iota(jnp.int32, (PEERS, R), 1)
    extra = [jnp.zeros((PEERS, R), F32) for _ in range(3)]
    for which, rows in enumerate((rows_two, rows_three)):
        packed, diagonal = packed_gram(rows)
        for part, values in enumerate(three(packed)):
            for m in range(4):
                put(wide, 12 * which + 4 * part + m, ROWS0, values[32 * m : 32 * m + 32, :])
        for part, values in enumerate(three(diagonal)):
            for m in range(4):
                extra[part] = jnp.where(
                    lane == 128 + 4 * which + m, values[32 * m : 32 * m + 32, :], extra[part]
                )
    pieces = rows_two.astype(F32)
    for n in range(4):
        put(wide, 24 + n, ROWS0, pieces[32 * n : 32 * n + 32, :])
    put(wide, 28, ROWS0, rows_three.astype(F32))
    seconds = at[0]
    names = (seconds >> 4, seconds & 15, at[1])
    for part in range(3):
        spot[...] = extra[part]
        spot[:, 0:BLK] = jnp.broadcast_to(names[part].astype(F32), (PEERS, BLK))
        put(wide, 29 + part, ROWS0, spot[...])
    out_ref[...] = whole(wide).astype(BF16).reshape(PEERS, ROWS0, R)


def second_kernel(got_ref, out_ref, wide, slab):
    fill(wide, got_ref[...].reshape(PEERS * ROWS0, R).astype(F32))
    total = got_ref[0].astype(F32)
    for source in range(1, PEERS):
        total = total + got_ref[source].astype(F32)
    for i in range(2):
        for u in range(2):
            slab[64 * i + 32 * u : 64 * i + 32 * u + 32, :] = take(wide, 24 + 2 * u + i, ROWS0)
    slab[128:160, :] = take(wide, 28, ROWS0)
    chunks = [total[12 * w : 12 * w + 4] + total[12 * w + 4 : 12 * w + 8] + total[12 * w + 8 : 12 * w + 12] for w in range(2)]
    for w in range(2):
        for part, values in enumerate(three(chunks[w])):
            slab[160 + 12 * w + 4 * part : 164 + 12 * w + 4 * part, :] = values
    slab[184:192, :] = jnp.zeros((8, R), F32)
    for part, values in enumerate(three(total[29:30] + total[30:31] + total[31:32])):
        slab[184 + part : 185 + part, :] = values
    out_ref[...] = slab[...].astype(BF16)


def third_kernel(*refs):
    pieces = refs[:ZS]
    pick_two_ref, pick_left_ref, pick_right_ref, out_ref, wide = refs[ZS:]

    def table(start, stop):
        return jnp.concatenate([ref[start:stop, :] for ref in pieces], axis=0)

    for i in range(2):
        rows = jnp.dot(pick_two_ref[...], table(64 * i, 64 * i + 64), preferred_element_type=F32)
        for d in range(PEERS):
            wide[d * ROWS2 + BLK * i : d * ROWS2 + BLK * (i + 1), :] = rows[BLK * d : BLK * (d + 1)]
    for i, pick_ref in enumerate((pick_left_ref, pick_right_ref)):
        rows = jnp.dot(pick_ref[...], table(128, 160), preferred_element_type=F32)
        for d in range(PEERS):
            wide[d * ROWS2 + BLK * (2 + i) : d * ROWS2 + BLK * (3 + i), :] = rows[BLK * d : BLK * (d + 1)]
    total = pieces[0][160:, :].astype(F32)
    for ref in pieces[1:]:
        total = total + ref[160:, :].astype(F32)
    gram_two = total[0:4] + total[4:8] + total[8:12]
    gram_three = total[12:16] + total[16:20] + total[20:24]
    normal = three(gram_two * gram_three)
    diagonal = total[24:25] + total[25:26] + total[26:27]
    diagonal = three(diagonal[:, 128:132] * diagonal[:, 132:136])
    for part in range(3):
        wide[96 + 4 * part : 100 + 4 * part, :] = normal[part]
    wide[108:112, :] = jnp.zeros((4, R), F32)
    for part in range(3):
        wide[108 + part : 109 + part, 128:132] = diagonal[part]
    tail = wide[96:112, :]
    for d in range(1, PEERS):
        wide[d * ROWS2 + 96 : d * ROWS2 + 112, :] = tail
    out_ref[...] = wide[...].astype(BF16).reshape(PEERS, ROWS2, R)


def dot_high(a, b, dims=((1,), (0,))):
    return lax.dot_general(
        a, b, (dims, ((), ())), precision=lax.Precision.HIGHEST, preferred_element_type=F32
    )


def reciprocal(value):
    guess = pltpu.reciprocal(value, approx=True)
    return guess * (2.0 - value * guess)


def inverse_root(value):
    guess = lax.rsqrt(value)
    return guess * (1.5 - 0.5 * value * guess * guess)


def eliminate(matrix, down, along):
    size = R // 2
    count = size // 8
    identity = jnp.where(down == along, 1.0, 0.0).astype(F32)
    left = [matrix[8 * g : 8 * g + 8] for g in range(count)]
    right = [identity[8 * g : 8 * g + 8] for g in range(count)]
    sub = lax.broadcasted_iota(jnp.int32, (8, size), 0)

    def row(value, j):
        return jnp.broadcast_to(value[j : j + 1, :], (8, size))

    def columns(g, p):
        return [jnp.broadcast_to(left[g][:, 8 * p + j : 8 * p + j + 1], (8, size)) for j in range(8)]

    for p in range(count):
        pivots = []
        for g in range(p, count):
            spread = columns(g, p)
            new_left, new_right = left[g], right[g]
            for n in range(4):
                j = 2 * n
                if g == p:
                    across = [[row(spread[m], j + i) for m in range(8)] for i in range(2)]
                    a, b, d = across[0][j], across[0][j + 1], across[1][j + 1]
                    scale = reciprocal(a * d - b * b)
                    rows = [row(new_left, j), row(new_left, j + 1), row(new_right, j), row(new_right, j + 1)]
                    pivots.append((across, a, b, d, scale, rows))
                    if n == 3:
                        break
                    first = jnp.where(sub > j + 1, spread[j], 0.0)
                    second = jnp.where(sub > j + 1, spread[j + 1], 0.0)
                else:
                    across, a, b, d, scale, rows = pivots[n]
                    first, second = spread[j], spread[j + 1]
                one = (first * d - second * b) * scale
                two = (second * a - first * b) * scale
                for m in range(j + 2, 8):
                    spread[m] = spread[m] - (one * across[0][m] + two * across[1][m])
                new_left = new_left - (one * rows[0] + two * rows[1])
                new_right = new_right - (one * rows[2] + two * rows[3])
            left[g], right[g] = new_left, new_right
        yield
    left = jnp.concatenate(left, axis=0)
    right = jnp.concatenate(right, axis=0)
    main = jnp.sum(jnp.where(down == along, left, 0.0), axis=1, keepdims=True)
    below = jnp.sum(jnp.where(down == along + 1, left, 0.0), axis=1, keepdims=True)
    above = pltpu.roll(jnp.broadcast_to(main, (size, size)), 1, 0)[:, :1]
    odd = lax.broadcasted_iota(jnp.int32, (size, 1), 0) % 2 == 1
    ratio = jnp.where(odd, below / above, 0.0)
    return (right - ratio * pltpu.roll(right, 1, 0)) * inverse_root(main - ratio * below)


def finish(steps):
    while True:
        try:
            next(steps)
        except StopIteration as stop:
            return stop.value


def scaled_normal(wide, down, along):
    half = R // 2
    packed, diagonal = [], []
    for m in range(4):
        rows = [take(wide, 96 + 4 * part + m, ROWS2) for part in range(3)]
        packed.append(rows[0] + rows[1] + rows[2])
        rows = [take(wide, 108 + part, ROWS2) for part in range(3)]
        diagonal.append((rows[0] + rows[1] + rows[2])[:, 128 + m : 129 + m])
    packed = jnp.concatenate(packed, axis=0)
    diagonal = jnp.concatenate(diagonal, axis=0)
    mixed = packed[:, :half]
    flipped = mixed.T
    upper = jnp.where(down >= along, mixed, flipped)
    corner = jnp.where(down == along, diagonal, jnp.where(down < along, mixed, flipped))
    scales = [
        [inverse_root(jnp.sum(jnp.where(down == along, part, 0.0), axis=axis, keepdims=True)) for axis in (1, 0)]
        for part in (upper, corner)
    ]
    upper = upper * scales[0][0] * scales[0][1]
    below = packed[:, half:] * scales[1][0] * scales[0][1]
    corner = corner * scales[1][0] * scales[1][1]
    return upper, below, corner, scales[0][1], scales[1][1]


def product_kernel(rows_ref, base_ref, tensor_ref, got_ref, out_ref, state_ref, wide, blocks, sems):
    def fetch(t):
        return pltpu.make_async_copy(tensor_ref.at[t], blocks.at[t], sems.at[t])

    for t in range(BLK):
        fetch(t).start()
    fill(wide, got_ref[...].reshape(PEERS * ROWS2, R).astype(F32))
    out_ref[...] = jnp.zeros_like(out_ref)
    half = R // 2
    down = lax.broadcasted_iota(jnp.int32, (half, half), 0)
    along = lax.broadcasted_iota(jnp.int32, (half, half), 1)
    upper, below, corner, scale, scale_last = scaled_normal(wide, down, along)
    steps = eliminate(upper, down, along)

    def one_block(t):
        left = [take(wide, BLK * i + t, ROWS2) for i in range(2)]
        right = jnp.concatenate([take(wide, BLK * (2 + i) + t, ROWS2) for i in range(2)], axis=0)
        right = right.astype(BF16)

        total = jnp.zeros((BS, R), F32)
        for q in range(BS // 4):
            parts = []
            for b in range(4 * q, 4 * q + 4):
                row = left[b // 32][b % 32 : b % 32 + 1, :]
                row = jnp.broadcast_to(row, (16, R)).astype(BF16)
                parts.append(jnp.concatenate([row] * 4, axis=0) * right)
            total = total + jnp.dot(
                blocks[t, :, 256 * q : 256 * q + 256],
                jnp.concatenate(parts, axis=0),
                preferred_element_type=F32,
            )
        place = pl.multiple_of((rows_ref[t] - base_ref[0]) * BS, BS)
        out_ref[pl.ds(place, BS), :] += total

    taken = 0
    for t in range(BLK):
        if t % 4 == 0:
            for later in range(t, t + 4):
                fetch(later).wait()
        one_block(t)
        while taken < min(half // 8, (t + 1) * half // 8 // (BLK - 4)):
            next(steps)
            taken += 1
    first = finish(steps)
    lower = dot_high(below, first, ((1,), (1,)))
    state_ref[0] = first
    state_ref[1] = corner - dot_high(lower, lower, ((1,), (1,)))
    state_ref[2] = dot_high(lower, first)
    state_ref[3] = jnp.broadcast_to(scale, (half, half))
    state_ref[4] = jnp.broadcast_to(scale_last, (half, half))


def products(block_rows, base, tensor_blocks, got):
    return call(
        product_kernel,
        (
            jax.ShapeDtypeStruct((XS * BS, R), F32),
            jax.ShapeDtypeStruct((5, R // 2, R // 2), F32),
        ),
        [SMEM, SMEM, HBM, VMEM],
        [
            halves(PEERS * ROWS2),
            pltpu.VMEM((BLK, BS, BS * BS), BF16),
            pltpu.SemaphoreType.DMA((BLK,)),
        ],
        cost_estimate=pl.CostEstimate(
            flops=2 * BLK * BS * BS * BS * R, bytes_accessed=BLK * BS * BS * BS * 2, transcendentals=0
        ),
    )(block_rows, base, tensor_blocks, got)


def inverse_kernel(state_ref, out_ref):
    half = R // 2
    down = lax.broadcasted_iota(jnp.int32, (half, half), 0)
    along = lax.broadcasted_iota(jnp.int32, (half, half), 1)
    scale, scale_last = state_ref[3, :1], state_ref[4, :1]
    last = finish(eliminate(state_ref[1], down, along))
    out_ref[:half, :half] = state_ref[0] * scale
    out_ref[:half, half:] = jnp.zeros((half, half), F32)
    out_ref[half:, :half] = -dot_high(last, state_ref[2]) * scale
    out_ref[half:, half:] = last * scale_last


def final_kernel(parts_ref, inverse_ref, out_ref):
    rows = (parts_ref[0] + parts_ref[1]) + (parts_ref[2] + parts_ref[3])
    inverse = inverse_ref[...]
    halfway = dot_high(rows, inverse, ((1,), (1,)))
    out_ref[...] = dot_high(halfway, inverse)


def body(tensor_blocks, block_rows, block_seconds, block_thirds, second_factor, third_factor):
    shape = jax.ShapeDtypeStruct
    exchange = functools.partial(lax.all_to_all, split_axis=0, concat_axis=0, tiled=True)
    x = lax.axis_index("x").astype(jnp.int32).reshape(1)
    wide_at = (lax.axis_index("y") * ZS + lax.axis_index("z")) * CS + lax.axis_index("c")
    base = (wide_at * XS).astype(jnp.int32).reshape(1)

    keep = functools.partial(pltpu.with_memory_space_constraint, memory_space=pltpu.HBM)
    sent = call(
        first_kernel,
        shape((PEERS, ROWS0, R), BF16),
        [SMEM, HBM, HBM, HBM, HBM],
        [
            halves(PEERS * ROWS0),
            pltpu.VMEM((PEERS, R), F32),
            pltpu.VMEM((128, R), BF16),
            pltpu.VMEM((32, R), BF16),
            pltpu.VMEM((2, 1, BLK), jnp.int32),
            pltpu.SemaphoreType.DMA((4,)),
        ],
    )(x, *map(keep, (second_factor, third_factor, block_seconds.reshape(1, BLK), block_thirds.reshape(1, BLK))))
    got0 = exchange(sent, RING)

    sent = call(
        second_kernel,
        shape((ROWS1, R), BF16),
        [VMEM],
        [halves(PEERS * ROWS0), pltpu.VMEM((ROWS1, R), F32)],
    )(got0)
    around = [[(z, (z + step) % ZS) for z in range(ZS)] for step in (1, -1)]
    from_low, from_high = [sent], [sent]
    for _ in range(3):
        from_low.append(lax.ppermute(from_low[-1], "z", around[0]))
        from_high.append(lax.ppermute(from_high[-1], "z", around[1]))
    pieces = from_low + from_high[1:] + [lax.ppermute(from_low[-1], "z", around[0])]

    names = got0[:, 29:32, :BLK].astype(jnp.int32)
    seconds = (names[:, 0] * 16 + names[:, 1]).reshape(-1)
    thirds = names[:, 2].reshape(-1)

    def source(holder):
        back = (lax.axis_index("z") - holder // CS) % ZS
        return (holder // (ZS * CS)) * CS + holder % CS, jnp.where(back < 4, back, 11 - back)

    pair, plane = source(seconds // 8)
    place_two = plane * 64 + seconds % 2 * 32 + pair * XS + seconds % 8 // 2
    pair, plane = source(thirds // 2)
    place_three = plane * 32 + pair * XS + thirds % 2 * 2

    def one_hot(place, width):
        return (place[:, None] == jnp.arange(width)[None, :]).astype(BF16)

    sent = call(
        third_kernel,
        shape((PEERS, ROWS2, R), BF16),
        [VMEM] * (ZS + 3),
        [pltpu.VMEM((PEERS * ROWS2, R), F32)],
    )(*pieces, one_hot(place_two, 64 * ZS), one_hot(place_three, 32 * ZS), one_hot(place_three + 1, 32 * ZS))
    got2 = exchange(sent, RING)

    summed, state = products(block_rows, base, tensor_blocks, got2)
    parts = exchange(summed.reshape(XS, BS, R), "x")
    inverse = call(
        inverse_kernel,
        shape((R, R), F32),
        [VMEM],
        cost_estimate=pl.CostEstimate(flops=10**9, bytes_accessed=10**6, transcendentals=0),
    )(state)
    return call(final_kernel, shape((BS, R), F32), [VMEM] * 2)(parts, inverse)


def solution(mesh):
    fine = Mesh(mesh.devices.reshape(YS, ZS, CS, XS), ("y", "z", "c", "x"))
    wide, every = ("y", "z", "c"), ("y", "z", "c", "x")
    in_specs = (
        P(every, None, None),
        P(every),
        P(every),
        P(every),
        P(wide, None),
        P(wide, None),
    )
    return jax.shard_map(body, mesh=fine, in_specs=in_specs, out_specs=P(every, None), check_vma=False)
```

```python
import functools
import jax
import jax.numpy as jnp
from jax import lax
from jax.experimental import pallas as pl
from jax.experimental.pallas import tpu as pltpu
from jax.sharding import Mesh, PartitionSpec as P

BS = 64
R = 256
BLK = 24
YS, ZS, CS, XS = 4, 8, 2, 4
PEERS = YS * CS * XS
RING = ("y", "c", "x")
PAIRS = YS * CS
ROWS0 = 48
ROWS1 = 192
ROWS2 = 112
F32 = jnp.float32
BF16 = jnp.bfloat16
VMEM = pl.BlockSpec(memory_space=pltpu.VMEM)
SMEM = pl.BlockSpec(memory_space=pltpu.SMEM)
HBM = pl.BlockSpec(memory_space=pltpu.HBM)
LIMIT = 48 * 1024 * 1024


def call(kernel, out_shape, in_specs, scratch=(), out_spec=VMEM, **kw):
    return pl.pallas_call(
        kernel,
        out_shape=out_shape,
        in_specs=in_specs,
        out_specs=jax.tree.map(lambda _: out_spec, out_shape),
        scratch_shapes=list(scratch),
        compiler_params=pltpu.CompilerParams(vmem_limit_bytes=LIMIT),
        **kw,
    )


def three(value):
    high = value.astype(BF16).astype(F32)
    rest = value - high
    middle = rest.astype(BF16).astype(F32)
    return high, middle, rest - middle


def halves(rows):
    return pltpu.VMEM((2, rows, 128), F32)


def put(wide, start, stride, values):
    for half in range(2):
        wide[half, pl.ds(start, values.shape[0], stride=stride), :] = values[:, 128 * half : 128 * half + 128]


def take(wide, start, stride, count=PEERS):
    return jnp.concatenate([wide[half, pl.ds(start, count, stride=stride), :] for half in range(2)], axis=1)


def fill(wide, values, start=0):
    for half in range(2):
        wide[half, start : start + values.shape[0]] = values[:, 128 * half : 128 * half + 128]


def whole(wide):
    return jnp.concatenate([wide[half] for half in range(2)], axis=1)


def packed_gram(rows):
    gram = lax.dot_general(rows, rows, (((0,), (0,)), ((), ())), preferred_element_type=F32)
    half = R // 2
    down = lax.broadcasted_iota(jnp.int32, (half, half), 0)
    along = lax.broadcasted_iota(jnp.int32, (half, half), 1)
    corner = gram[half:, half:]
    mixed = jnp.where(down >= along, gram[:half, :half], corner)
    diagonal = jnp.sum(jnp.where(down == along, corner, 0.0), axis=1, keepdims=True)
    return jnp.concatenate([mixed, gram[half:, :half]], axis=1), diagonal


def first_kernel(x_ref, second_ref, third_ref, seconds_ref, thirds_ref, out_ref, wide, table, two, few, at, sems):
    x = x_ref[0]
    copies = [
        pltpu.make_async_copy(second_ref, two, sems.at[0]),
        pltpu.make_async_copy(third_ref, few, sems.at[1]),
        pltpu.make_async_copy(seconds_ref, at.at[0], sems.at[2]),
        pltpu.make_async_copy(thirds_ref, at.at[1], sems.at[3]),
    ]
    for copy in copies:
        copy.start()
    for copy in copies:
        copy.wait()

    def mine(start):
        return take(table, start + x, XS, PAIRS)

    fill(table, two[...].astype(F32))
    fill(table, few[...].astype(F32), 512)
    for n in range(20):
        put(wide, 24 + n, ROWS0, mine(32 * n))
    grams = [packed_gram(two[...]), packed_gram(few[...])]
    lane = lax.broadcasted_iota(jnp.int32, (128, R), 1)
    column = jnp.where(lane < 132, grams[0][1], grams[1][1])
    for part, values in enumerate(three(column)):
        fill(table, values, 128 * part)
    lane = lane[:PAIRS]
    seconds = at[0]
    names = (seconds >> 4, seconds & 15, at[1])
    for part in range(3):
        extra = jnp.zeros((PAIRS, R), F32)
        for m in range(4):
            extra = jnp.where((lane == 128 + m) | (lane == 132 + m), mine(128 * part + 32 * m), extra)
        put(wide, 44 + part, ROWS0, extra)
        wide[0, pl.ds(44 + part, PAIRS, stride=ROWS0), :] = jnp.concatenate(
            [jnp.broadcast_to(names[part].astype(F32), (PAIRS, BLK)), jnp.zeros((PAIRS, 128 - BLK), F32)], axis=1
        )
    put(wide, 47, ROWS0, jnp.zeros((PAIRS, R), F32))
    for which in range(2):
        for part, values in enumerate(three(grams[which][0])):
            fill(table, values, 128 * part)
            for m in range(4):
                put(wide, 12 * which + 4 * part + m, ROWS0, mine(128 * part + 32 * m))
    out_ref[...] = whole(wide).astype(BF16).reshape(PAIRS, ROWS0, R)


def second_kernel(z_ref, got_ref, out_ref, places_ref, wide, slab):
    fill(wide, got_ref[...].reshape(PAIRS * ROWS0, R).astype(F32))
    total = got_ref[0].astype(F32)
    for source in range(1, PAIRS):
        total = total + got_ref[source].astype(F32)
    for i in range(2):
        for block in range(8):
            slab[64 * i + 8 * block : 64 * i + 8 * block + 8, :] = take(wide, 24 + 2 * block + i, ROWS0, PAIRS)
    for n in range(4):
        slab[128 + 8 * n : 136 + 8 * n, :] = take(wide, 40 + n, ROWS0, PAIRS)
    chunks = [total[12 * w : 12 * w + 4] + total[12 * w + 4 : 12 * w + 8] + total[12 * w + 8 : 12 * w + 12] for w in range(2)]
    for w in range(2):
        for part, values in enumerate(three(chunks[w])):
            slab[160 + 12 * w + 4 * part : 164 + 12 * w + 4 * part, :] = values
    slab[184:192, :] = jnp.zeros((8, R), F32)
    for part, values in enumerate(three(total[44:45] + total[45:46] + total[46:47])):
        slab[184 + part : 185 + part, :] = values
    out_ref[...] = slab[...].astype(BF16)

    names = [take(wide, 44 + n, ROWS0, PAIRS)[:, :128].astype(jnp.int32) for n in range(3)]
    seconds, thirds = names[0] * 16 + names[1], names[2]

    def source(holder):
        back = (z_ref[0] - (holder >> 1)) & (ZS - 1)
        return ((holder >> 4) << 1) | (holder & 1), jnp.where(back < 4, back, 11 - back)

    pair, plane = source(seconds >> 3)
    place_two = plane * 64 + (seconds & 7) * PAIRS + pair
    pair, plane = source(thirds >> 1)
    place_three = plane * 32 + (thirds & 1) * (2 * PAIRS) + pair
    places_ref[:PAIRS] = place_two
    places_ref[PAIRS:] = place_three


def third_kernel(*refs):
    pieces = refs[:ZS]
    pick_two_ref, pick_left_ref, pick_right_ref, out_ref, wide, narrow, sems = refs[ZS:]

    def table(start, stop):
        return jnp.concatenate([ref[start:stop, :] for ref in pieces], axis=0)

    for i in range(2):
        rows = jnp.dot(pick_two_ref[...], table(64 * i, 64 * i + 64), preferred_element_type=F32)
        for d in range(PEERS):
            wide[d * ROWS2 + BLK * i : d * ROWS2 + BLK * (i + 1), :] = rows[BLK * d : BLK * (d + 1)]
    for i, pick_ref in enumerate((pick_left_ref, pick_right_ref)):
        rows = jnp.dot(pick_ref[...], table(128, 160), preferred_element_type=F32)
        for d in range(PEERS):
            wide[d * ROWS2 + BLK * (2 + i) : d * ROWS2 + BLK * (3 + i), :] = rows[BLK * d : BLK * (d + 1)]
    total = pieces[0][160:, :].astype(F32)
    for ref in pieces[1:]:
        total = total + ref[160:, :].astype(F32)
    gram_two = total[0:4] + total[4:8] + total[8:12]
    gram_three = total[12:16] + total[16:20] + total[20:24]
    normal = three(gram_two * gram_three)
    diagonal = total[24:25] + total[25:26] + total[26:27]
    diagonal = three(diagonal[:, 128:132] * diagonal[:, 132:136])
    for part in range(3):
        wide[96 + 4 * part : 100 + 4 * part, :] = normal[part]
    wide[108:112, :] = jnp.zeros((4, R), F32)
    for part in range(3):
        wide[108 + part : 109 + part, 128:132] = diagonal[part]
    tail = wide[96:112, :]
    for d in range(1, PEERS):
        wide[d * ROWS2 + 96 : d * ROWS2 + 112, :] = tail
    copies = []
    for n in range(4):
        peers = pl.ds(8 * n, 8)
        rows = wide[8 * n * ROWS2 : 8 * (n + 1) * ROWS2, :]
        narrow[peers] = rows.astype(BF16).reshape(8, ROWS2, R)
        copies.append(pltpu.make_async_copy(narrow.at[peers], out_ref.at[peers], sems.at[n]))
        copies[-1].start()
    for copy in copies:
        copy.wait()


def dot_high(a, b, dims=((1,), (0,))):
    return lax.dot_general(
        a, b, (dims, ((), ())), precision=lax.Precision.HIGHEST, preferred_element_type=F32
    )


def reciprocal(value):
    guess = pltpu.reciprocal(value, approx=True)
    return guess * (2.0 - value * guess)


def inverse_root(value):
    guess = lax.rsqrt(value)
    return guess * (1.5 - 0.5 * value * guess * guess)


def eliminate(matrix, down, along):
    size = R // 2
    count = size // 8
    identity = jnp.where(down == along, 1.0, 0.0).astype(F32)
    left = [matrix[8 * g : 8 * g + 8] for g in range(count)]
    right = [identity[8 * g : 8 * g + 8] for g in range(count)]
    sub = lax.broadcasted_iota(jnp.int32, (8, size), 0)

    def row(value, j):
        return jnp.broadcast_to(value[j : j + 1, :], (8, size))

    def columns(g, p):
        return [jnp.broadcast_to(left[g][:, 8 * p + j : 8 * p + j + 1], (8, size)) for j in range(8)]

    for p in range(count):
        pivots = []
        for g in range(p, count):
            spread = columns(g, p)
            new_left, new_right = left[g], right[g]
            for n in range(4):
                j = 2 * n
                if g == p:
                    across = [[row(spread[m], j + i) for m in range(8)] for i in range(2)]
                    a, b, d = across[0][j], across[0][j + 1], across[1][j + 1]
                    scale = reciprocal(a * d - b * b)
                    rows = [row(new_left, j), row(new_left, j + 1), row(new_right, j), row(new_right, j + 1)]
                    pivots.append((across, a, b, d, scale, rows))
                    if n == 3:
                        break
                    first = jnp.where(sub > j + 1, spread[j], 0.0)
                    second = jnp.where(sub > j + 1, spread[j + 1], 0.0)
                else:
                    across, a, b, d, scale, rows = pivots[n]
                    first, second = spread[j], spread[j + 1]
                one = (first * d - second * b) * scale
                two = (second * a - first * b) * scale
                for m in range(j + 2, 8):
                    spread[m] = spread[m] - (one * across[0][m] + two * across[1][m])
                new_left = new_left - (one * rows[0] + two * rows[1])
                new_right = new_right - (one * rows[2] + two * rows[3])
            left[g], right[g] = new_left, new_right
        yield
    left = jnp.concatenate(left, axis=0)
    right = jnp.concatenate(right, axis=0)
    main = jnp.sum(jnp.where(down == along, left, 0.0), axis=1, keepdims=True)
    below = jnp.sum(jnp.where(down == along + 1, left, 0.0), axis=1, keepdims=True)
    above = pltpu.roll(jnp.broadcast_to(main, (size, size)), 1, 0)[:, :1]
    odd = lax.broadcasted_iota(jnp.int32, (size, 1), 0) % 2 == 1
    ratio = jnp.where(odd, below / above, 0.0)
    return (right - ratio * pltpu.roll(right, 1, 0)) * inverse_root(main - ratio * below)


def finish(steps):
    while True:
        try:
            next(steps)
        except StopIteration as stop:
            return stop.value


def scaled_normal(wide, down, along):
    half = R // 2
    packed, diagonal = [], []
    for m in range(4):
        rows = [take(wide, 96 + 4 * part + m, ROWS2) for part in range(3)]
        packed.append(rows[0] + rows[1] + rows[2])
        rows = [take(wide, 108 + part, ROWS2) for part in range(3)]
        diagonal.append((rows[0] + rows[1] + rows[2])[:, 128 + m : 129 + m])
    packed = jnp.concatenate(packed, axis=0)
    diagonal = jnp.concatenate(diagonal, axis=0)
    mixed = packed[:, :half]
    flipped = mixed.T
    upper = jnp.where(down >= along, mixed, flipped)
    corner = jnp.where(down == along, diagonal, jnp.where(down < along, mixed, flipped))
    scales = [
        [inverse_root(jnp.sum(jnp.where(down == along, part, 0.0), axis=axis, keepdims=True)) for axis in (1, 0)]
        for part in (upper, corner)
    ]
    upper = upper * scales[0][0] * scales[0][1]
    below = packed[:, half:] * scales[1][0] * scales[0][1]
    corner = corner * scales[1][0] * scales[1][1]
    return upper, below, corner, scales[0][1], scales[1][1]


def product_kernel(rows_ref, base_ref, tensor_ref, got_ref, out_ref, state_ref, wide, blocks, sems):
    def fetch(t):
        return pltpu.make_async_copy(tensor_ref.at[t], blocks.at[t], sems.at[t])

    for t in range(BLK):
        fetch(t).start()
    fill(wide, got_ref[...].reshape(PEERS * ROWS2, R).astype(F32))
    out_ref[...] = jnp.zeros_like(out_ref)
    half = R // 2
    down = lax.broadcasted_iota(jnp.int32, (half, half), 0)
    along = lax.broadcasted_iota(jnp.int32, (half, half), 1)
    upper, below, corner, scale, scale_last = scaled_normal(wide, down, along)
    steps = eliminate(upper, down, along)

    def one_block(t):
        left = [take(wide, BLK * i + t, ROWS2) for i in range(2)]
        right = jnp.concatenate([take(wide, BLK * (2 + i) + t, ROWS2) for i in range(2)], axis=0)
        right = right.astype(BF16)

        total = jnp.zeros((BS, R), F32)
        for q in range(BS // 4):
            parts = []
            for b in range(4 * q, 4 * q + 4):
                row = left[b // 32][b % 32 : b % 32 + 1, :]
                row = jnp.broadcast_to(row, (16, R)).astype(BF16)
                parts.append(jnp.concatenate([row] * 4, axis=0) * right)
            total = total + jnp.dot(
                blocks[t, :, 256 * q : 256 * q + 256],
                jnp.concatenate(parts, axis=0),
                preferred_element_type=F32,
            )
        place = pl.multiple_of((rows_ref[t] - base_ref[0]) * BS, BS)
        out_ref[pl.ds(place, BS), :] += total

    taken = 0
    for t in range(BLK):
        for later in range(t, {0: 4, 4: 12, 12: BLK}.get(t, t)):
            fetch(later).wait()
        one_block(t)
        while taken < min(half // 8, (t + 1) * half // 8 // (BLK - 4)):
            next(steps)
            taken += 1
    first = finish(steps)
    lower = dot_high(below, first, ((1,), (1,)))
    state_ref[0] = first
    state_ref[1] = corner - dot_high(lower, lower, ((1,), (1,)))
    state_ref[2] = dot_high(lower, first)
    state_ref[3] = jnp.broadcast_to(scale, (half, half))
    state_ref[4] = jnp.broadcast_to(scale_last, (half, half))


def products(block_rows, base, tensor_blocks, got):
    return call(
        product_kernel,
        (
            jax.ShapeDtypeStruct((XS * BS, R), F32),
            jax.ShapeDtypeStruct((5, R // 2, R // 2), F32),
        ),
        [SMEM, SMEM, HBM, VMEM],
        [
            halves(PEERS * ROWS2),
            pltpu.VMEM((BLK, BS, BS * BS), BF16),
            pltpu.SemaphoreType.DMA((BLK,)),
        ],
        cost_estimate=pl.CostEstimate(
            flops=2 * BLK * BS * BS * BS * R, bytes_accessed=BLK * BS * BS * BS * 2, transcendentals=0
        ),
    )(block_rows, base, tensor_blocks, got)


def inverse_kernel(state_ref, out_ref):
    half = R // 2
    down = lax.broadcasted_iota(jnp.int32, (half, half), 0)
    along = lax.broadcasted_iota(jnp.int32, (half, half), 1)
    scale, scale_last = state_ref[3, :1], state_ref[4, :1]
    last = finish(eliminate(state_ref[1], down, along))
    out_ref[:half, :half] = state_ref[0] * scale
    out_ref[:half, half:] = jnp.zeros((half, half), F32)
    out_ref[half:, :half] = -dot_high(last, state_ref[2]) * scale
    out_ref[half:, half:] = last * scale_last


def final_kernel(parts_ref, inverse_ref, out_ref):
    rows = (parts_ref[0] + parts_ref[1]) + (parts_ref[2] + parts_ref[3])
    inverse = inverse_ref[...]
    halfway = dot_high(rows, inverse, ((1,), (1,)))
    out_ref[...] = dot_high(halfway, inverse)


def body(tensor_blocks, block_rows, block_seconds, block_thirds, second_factor, third_factor):
    shape = jax.ShapeDtypeStruct
    exchange = functools.partial(lax.all_to_all, split_axis=0, concat_axis=0, tiled=True)
    x = lax.axis_index("x").astype(jnp.int32).reshape(1)
    wide_at = (lax.axis_index("y") * ZS + lax.axis_index("z")) * CS + lax.axis_index("c")
    base = (wide_at * XS).astype(jnp.int32).reshape(1)

    keep = functools.partial(pltpu.with_memory_space_constraint, memory_space=pltpu.HBM)
    sent = call(
        first_kernel,
        pltpu.HBM((PAIRS, ROWS0, R), BF16),
        [SMEM, HBM, HBM, HBM, HBM],
        [
            halves(PAIRS * ROWS0),
            halves(640),
            pltpu.VMEM((512, R), BF16),
            pltpu.VMEM((128, R), BF16),
            pltpu.VMEM((2, 1, BLK), jnp.int32),
            pltpu.SemaphoreType.DMA((4,)),
        ],
    )(x, *map(keep, (second_factor, third_factor, block_seconds.reshape(1, BLK), block_thirds.reshape(1, BLK))))
    got0 = exchange(sent, ("y", "c"))

    z = lax.axis_index("z").astype(jnp.int32).reshape(1)
    sent, places = call(
        second_kernel,
        (shape((ROWS1, R), BF16), shape((2 * PAIRS, 128), jnp.int32)),
        [SMEM, VMEM],
        [halves(PAIRS * ROWS0), pltpu.VMEM((ROWS1, R), F32)],
    )(z, got0)
    around = [[(z, (z + step) % ZS) for z in range(ZS)] for step in (1, -1)]
    from_low, from_high = [sent], [sent]
    for _ in range(3):
        from_low.append(lax.ppermute(from_low[-1], "z", around[0]))
        from_high.append(lax.ppermute(from_high[-1], "z", around[1]))
    pieces = from_low + from_high[1:] + [lax.ppermute(from_low[-1], "z", around[0])]

    others = [
        lax.ppermute(places, "x", [(n, (n + step) % XS) for n in range(XS)]) for step in (3, 2, 1)
    ]
    places = jnp.stack([*others, places] * 2)
    places = lax.dynamic_slice_in_dim(places, XS - 1 - lax.axis_index("x"), XS, 0)[:, :, :BLK]
    place_two = places[:, :PAIRS].swapaxes(0, 1).reshape(-1)
    place_three = places[:, PAIRS:].swapaxes(0, 1).reshape(-1)

    def one_hot(place, width):
        return (place[:, None] == jnp.arange(width)[None, :]).astype(BF16)

    sent = call(
        third_kernel,
        pltpu.HBM((PEERS, ROWS2, R), BF16),
        [VMEM] * (ZS + 3),
        [
            pltpu.VMEM((PEERS * ROWS2, R), F32),
            pltpu.VMEM((PEERS, ROWS2, R), BF16),
            pltpu.SemaphoreType.DMA((4,)),
        ],
        HBM,
    )(*pieces, one_hot(place_two, 64 * ZS), one_hot(place_three, 32 * ZS), one_hot(place_three + PAIRS, 32 * ZS))
    got2 = exchange(sent, RING)

    summed, state = products(block_rows, base, tensor_blocks, got2)
    parts = exchange(summed.reshape(XS, BS, R), "x")
    inverse = call(
        inverse_kernel,
        shape((R, R), F32),
        [VMEM],
        cost_estimate=pl.CostEstimate(flops=10**9, bytes_accessed=10**6, transcendentals=0),
    )(state)
    return call(final_kernel, shape((BS, R), F32), [VMEM] * 2)(parts, inverse)


def solution(mesh):
    fine = Mesh(mesh.devices.reshape(YS, ZS, CS, XS), ("y", "z", "c", "x"))
    wide, every = ("y", "z", "c"), ("y", "z", "c", "x")
    in_specs = (
        P(every, None, None),
        P(every),
        P(every),
        P(every),
        P(wide, None),
        P(wide, None),
    )
    return jax.shard_map(body, mesh=fine, in_specs=in_specs, out_specs=P(every, None), check_vma=False)
```

```python
import functools
import jax
import jax.numpy as jnp
from jax import lax
from jax.experimental import pallas as pl
from jax.experimental.pallas import tpu as pltpu
from jax.sharding import Mesh, PartitionSpec as P

BS = 64
R = 256
BLK = 24
YS, ZS, CS, XS = 4, 8, 2, 4
PEERS = YS * CS * XS
RING = ("y", "c", "x")
PAIRS = YS * CS
ROWS0 = 48
ROWS1 = 192
ROWS2 = 112
F32 = jnp.float32
BF16 = jnp.bfloat16
VMEM = pl.BlockSpec(memory_space=pltpu.VMEM)
SMEM = pl.BlockSpec(memory_space=pltpu.SMEM)
HBM = pl.BlockSpec(memory_space=pltpu.HBM)
LIMIT = 48 * 1024 * 1024


def call(kernel, out_shape, in_specs, scratch=(), out_spec=VMEM, **kw):
    return pl.pallas_call(
        kernel,
        out_shape=out_shape,
        in_specs=in_specs,
        out_specs=jax.tree.map(lambda _: out_spec, out_shape),
        scratch_shapes=list(scratch),
        compiler_params=pltpu.CompilerParams(vmem_limit_bytes=LIMIT),
        **kw,
    )


def three(value):
    high = value.astype(BF16).astype(F32)
    rest = value - high
    middle = rest.astype(BF16).astype(F32)
    return high, middle, rest - middle


def halves(rows):
    return pltpu.VMEM((2, rows, 128), F32)


def put(wide, start, stride, values):
    for half in range(2):
        wide[half, pl.ds(start, values.shape[0], stride=stride), :] = values[:, 128 * half : 128 * half + 128]


def take(wide, start, stride, count=PEERS):
    return jnp.concatenate([wide[half, pl.ds(start, count, stride=stride), :] for half in range(2)], axis=1)


def fill(wide, values, start=0):
    for half in range(2):
        wide[half, start : start + values.shape[0]] = values[:, 128 * half : 128 * half + 128]


def whole(wide):
    return jnp.concatenate([wide[half] for half in range(2)], axis=1)


def packed_gram(rows):
    gram = lax.dot_general(rows, rows, (((0,), (0,)), ((), ())), preferred_element_type=F32)
    half = R // 2
    down = lax.broadcasted_iota(jnp.int32, (half, half), 0)
    along = lax.broadcasted_iota(jnp.int32, (half, half), 1)
    corner = gram[half:, half:]
    mixed = jnp.where(down >= along, gram[:half, :half], corner)
    diagonal = jnp.sum(jnp.where(down == along, corner, 0.0), axis=1, keepdims=True)
    return jnp.concatenate([mixed, gram[half:, :half]], axis=1), diagonal


def first_kernel(x_ref, second_ref, third_ref, seconds_ref, thirds_ref, out_ref, wide, table, two, few, at, sems):
    x = x_ref[0]
    copies = [
        pltpu.make_async_copy(second_ref, two, sems.at[0]),
        pltpu.make_async_copy(third_ref, few, sems.at[1]),
        pltpu.make_async_copy(seconds_ref, at.at[0], sems.at[2]),
        pltpu.make_async_copy(thirds_ref, at.at[1], sems.at[3]),
    ]
    for copy in copies:
        copy.start()
    for copy in copies:
        copy.wait()

    def mine(start):
        return take(table, start + x, XS, PAIRS)

    fill(table, two[...].astype(F32))
    fill(table, few[...].astype(F32), 512)
    for n in range(20):
        put(wide, 24 + n, ROWS0, mine(32 * n))
    grams = [packed_gram(two[...]), packed_gram(few[...])]
    lane = lax.broadcasted_iota(jnp.int32, (128, R), 1)
    column = jnp.where(lane < 132, grams[0][1], grams[1][1])
    for part, values in enumerate(three(column)):
        fill(table, values, 128 * part)
    lane = lane[:PAIRS]
    seconds = at[0]
    names = (seconds >> 4, seconds & 15, at[1])
    for part in range(3):
        extra = jnp.zeros((PAIRS, R), F32)
        for m in range(4):
            extra = jnp.where((lane == 128 + m) | (lane == 132 + m), mine(128 * part + 32 * m), extra)
        put(wide, 44 + part, ROWS0, extra)
        wide[0, pl.ds(44 + part, PAIRS, stride=ROWS0), :] = jnp.concatenate(
            [jnp.broadcast_to(names[part].astype(F32), (PAIRS, BLK)), jnp.zeros((PAIRS, 128 - BLK), F32)], axis=1
        )
    put(wide, 47, ROWS0, jnp.zeros((PAIRS, R), F32))
    for which in range(2):
        for part, values in enumerate(three(grams[which][0])):
            fill(table, values, 128 * part)
            for m in range(4):
                put(wide, 12 * which + 4 * part + m, ROWS0, mine(128 * part + 32 * m))
    out_ref[...] = whole(wide).astype(BF16).reshape(PAIRS, ROWS0, R)


def second_kernel(z_ref, got_ref, out_ref, places_ref, wide, slab):
    fill(wide, got_ref[...].reshape(PAIRS * ROWS0, R).astype(F32))
    total = got_ref[0].astype(F32)
    for source in range(1, PAIRS):
        total = total + got_ref[source].astype(F32)
    for i in range(2):
        for block in range(8):
            slab[64 * i + 8 * block : 64 * i + 8 * block + 8, :] = take(wide, 24 + 2 * block + i, ROWS0, PAIRS)
    for n in range(4):
        slab[128 + 8 * n : 136 + 8 * n, :] = take(wide, 40 + n, ROWS0, PAIRS)
    chunks = [total[12 * w : 12 * w + 4] + total[12 * w + 4 : 12 * w + 8] + total[12 * w + 8 : 12 * w + 12] for w in range(2)]
    for w in range(2):
        for part, values in enumerate(three(chunks[w])):
            slab[160 + 12 * w + 4 * part : 164 + 12 * w + 4 * part, :] = values
    slab[184:192, :] = jnp.zeros((8, R), F32)
    for part, values in enumerate(three(total[44:45] + total[45:46] + total[46:47])):
        slab[184 + part : 185 + part, :] = values
    out_ref[...] = slab[...].astype(BF16)

    names = [take(wide, 44 + n, ROWS0, PAIRS)[:, :128].astype(jnp.int32) for n in range(3)]
    seconds, thirds = names[0] * 16 + names[1], names[2]

    def source(holder):
        back = (z_ref[0] - (holder >> 1)) & (ZS - 1)
        return ((holder >> 4) << 1) | (holder & 1), jnp.where(back < 4, back, 11 - back)

    pair, plane = source(seconds >> 3)
    place_two = plane * 64 + (seconds & 7) * PAIRS + pair
    pair, plane = source(thirds >> 1)
    place_three = plane * 32 + (thirds & 1) * (2 * PAIRS) + pair
    places_ref[:PAIRS] = place_two
    places_ref[PAIRS:] = place_three


def third_kernel(*refs):
    pieces = refs[:ZS]
    pick_two_ref, pick_left_ref, pick_right_ref, out_ref, wide, narrow, sems = refs[ZS:]

    def table(start, stop):
        return jnp.concatenate([ref[start:stop, :] for ref in pieces], axis=0)

    for i in range(2):
        rows = jnp.dot(pick_two_ref[...], table(64 * i, 64 * i + 64), preferred_element_type=F32)
        for d in range(PEERS):
            wide[d * ROWS2 + BLK * i : d * ROWS2 + BLK * (i + 1), :] = rows[BLK * d : BLK * (d + 1)]
    for i, pick_ref in enumerate((pick_left_ref, pick_right_ref)):
        rows = jnp.dot(pick_ref[...], table(128, 160), preferred_element_type=F32)
        for d in range(PEERS):
            wide[d * ROWS2 + BLK * (2 + i) : d * ROWS2 + BLK * (3 + i), :] = rows[BLK * d : BLK * (d + 1)]
    total = pieces[0][160:, :].astype(F32)
    for ref in pieces[1:]:
        total = total + ref[160:, :].astype(F32)
    gram_two = total[0:4] + total[4:8] + total[8:12]
    gram_three = total[12:16] + total[16:20] + total[20:24]
    normal = three(gram_two * gram_three)
    diagonal = total[24:25] + total[25:26] + total[26:27]
    diagonal = three(diagonal[:, 128:132] * diagonal[:, 132:136])
    for part in range(3):
        wide[96 + 4 * part : 100 + 4 * part, :] = normal[part]
    wide[108:112, :] = jnp.zeros((4, R), F32)
    for part in range(3):
        wide[108 + part : 109 + part, 128:132] = diagonal[part]
    tail = wide[96:112, :]
    for d in range(1, PEERS):
        wide[d * ROWS2 + 96 : d * ROWS2 + 112, :] = tail
    copies = []
    for n in range(4):
        peers = pl.ds(8 * n, 8)
        rows = wide[8 * n * ROWS2 : 8 * (n + 1) * ROWS2, :]
        narrow[peers] = rows.astype(BF16).reshape(8, ROWS2, R)
        copies.append(pltpu.make_async_copy(narrow.at[peers], out_ref.at[peers], sems.at[n]))
        copies[-1].start()
    for copy in copies:
        copy.wait()


def dot_high(a, b, dims=((1,), (0,))):
    return lax.dot_general(
        a, b, (dims, ((), ())), precision=lax.Precision.HIGHEST, preferred_element_type=F32
    )


def reciprocal(value):
    guess = pltpu.reciprocal(value, approx=True)
    return guess * (2.0 - value * guess)


def inverse_root(value):
    guess = lax.rsqrt(value)
    return guess * (1.5 - 0.5 * value * guess * guess)


def eliminate(matrix, down, along):
    size = R // 2
    count = size // 8
    identity = jnp.where(down == along, 1.0, 0.0).astype(F32)
    left = [matrix[8 * g : 8 * g + 8] for g in range(count)]
    right = [identity[8 * g : 8 * g + 8] for g in range(count)]
    sub = lax.broadcasted_iota(jnp.int32, (8, size), 0)

    def row(value, j):
        return jnp.broadcast_to(value[j : j + 1, :], (8, size))

    def columns(g, p):
        return [jnp.broadcast_to(left[g][:, 8 * p + j : 8 * p + j + 1], (8, size)) for j in range(8)]

    for p in range(count):
        pivots = []
        for g in range(p, count):
            spread = columns(g, p)
            new_left, new_right = left[g], right[g]
            for n in range(4):
                j = 2 * n
                if g == p:
                    across = [[row(spread[m], j + i) for m in range(8)] for i in range(2)]
                    a, b, d = across[0][j], across[0][j + 1], across[1][j + 1]
                    scale = reciprocal(a * d - b * b)
                    rows = [row(new_left, j), row(new_left, j + 1), row(new_right, j), row(new_right, j + 1)]
                    pivots.append((across, a, b, d, scale, rows))
                    if n == 3:
                        break
                    first = jnp.where(sub > j + 1, spread[j], 0.0)
                    second = jnp.where(sub > j + 1, spread[j + 1], 0.0)
                else:
                    across, a, b, d, scale, rows = pivots[n]
                    first, second = spread[j], spread[j + 1]
                one = (first * d - second * b) * scale
                two = (second * a - first * b) * scale
                for m in range(j + 2, 8):
                    spread[m] = spread[m] - (one * across[0][m] + two * across[1][m])
                new_left = new_left - (one * rows[0] + two * rows[1])
                new_right = new_right - (one * rows[2] + two * rows[3])
            left[g], right[g] = new_left, new_right
        yield
    left = jnp.concatenate(left, axis=0)
    right = jnp.concatenate(right, axis=0)
    main = jnp.sum(jnp.where(down == along, left, 0.0), axis=1, keepdims=True)
    below = jnp.sum(jnp.where(down == along + 1, left, 0.0), axis=1, keepdims=True)
    above = pltpu.roll(jnp.broadcast_to(main, (size, size)), 1, 0)[:, :1]
    odd = lax.broadcasted_iota(jnp.int32, (size, 1), 0) % 2 == 1
    ratio = jnp.where(odd, below / above, 0.0)
    return (right - ratio * pltpu.roll(right, 1, 0)) * inverse_root(main - ratio * below)


def finish(steps):
    while True:
        try:
            next(steps)
        except StopIteration as stop:
            return stop.value


def scaled_normal(wide, down, along):
    half = R // 2
    packed, diagonal = [], []
    for m in range(4):
        rows = [take(wide, 96 + 4 * part + m, ROWS2) for part in range(3)]
        packed.append(rows[0] + rows[1] + rows[2])
        rows = [take(wide, 108 + part, ROWS2) for part in range(3)]
        diagonal.append((rows[0] + rows[1] + rows[2])[:, 128 + m : 129 + m])
    packed = jnp.concatenate(packed, axis=0)
    diagonal = jnp.concatenate(diagonal, axis=0)
    mixed = packed[:, :half]
    flipped = mixed.T
    upper = jnp.where(down >= along, mixed, flipped)
    corner = jnp.where(down == along, diagonal, jnp.where(down < along, mixed, flipped))
    scales = [
        [inverse_root(jnp.sum(jnp.where(down == along, part, 0.0), axis=axis, keepdims=True)) for axis in (1, 0)]
        for part in (upper, corner)
    ]
    upper = upper * scales[0][0] * scales[0][1]
    below = packed[:, half:] * scales[1][0] * scales[0][1]
    corner = corner * scales[1][0] * scales[1][1]
    return upper, below, corner, scales[0][1], scales[1][1]


def product_kernel(rows_ref, base_ref, tensor_ref, got_ref, out_ref, state_ref, wide, blocks, sems):
    def fetch(t):
        return pltpu.make_async_copy(tensor_ref.at[t], blocks.at[t], sems.at[t])

    for t in range(BLK):
        fetch(t).start()
    fill(wide, got_ref[...].reshape(PEERS * ROWS2, R).astype(F32))
    out_ref[...] = jnp.zeros_like(out_ref)
    half = R // 2
    down = lax.broadcasted_iota(jnp.int32, (half, half), 0)
    along = lax.broadcasted_iota(jnp.int32, (half, half), 1)
    upper, below, corner, scale, scale_last = scaled_normal(wide, down, along)
    steps = eliminate(upper, down, along)

    def one_block(t):
        left = [take(wide, BLK * i + t, ROWS2) for i in range(2)]
        right = jnp.concatenate([take(wide, BLK * (2 + i) + t, ROWS2) for i in range(2)], axis=0)
        right = right.astype(BF16)

        total = jnp.zeros((BS, R), F32)
        for q in range(BS // 4):
            parts = []
            for b in range(4 * q, 4 * q + 4):
                row = left[b // 32][b % 32 : b % 32 + 1, :]
                row = jnp.broadcast_to(row, (16, R)).astype(BF16)
                parts.append(jnp.concatenate([row] * 4, axis=0) * right)
            total = total + jnp.dot(
                blocks[t, :, 256 * q : 256 * q + 256],
                jnp.concatenate(parts, axis=0),
                preferred_element_type=F32,
            )
        place = pl.multiple_of((rows_ref[t] - base_ref[0]) * BS, BS)
        out_ref[pl.ds(place, BS), :] += total

    taken = 0
    for t in range(BLK):
        for later in range(t, {0: 4, 4: 12, 12: BLK}.get(t, t)):
            fetch(later).wait()
        one_block(t)
        while taken < min(half // 8, (t + 1) * half // 8 // (BLK - 4)):
            next(steps)
            taken += 1
    first = finish(steps)
    lower = dot_high(below, first, ((1,), (1,)))
    state_ref[0] = first
    state_ref[1] = corner - dot_high(lower, lower, ((1,), (1,)))
    state_ref[2] = lower
    state_ref[3] = jnp.broadcast_to(scale, (half, half))
    state_ref[4] = jnp.broadcast_to(scale_last, (half, half))


def products(block_rows, base, tensor_blocks, got):
    return call(
        product_kernel,
        (
            jax.ShapeDtypeStruct((XS * BS, R), F32),
            jax.ShapeDtypeStruct((5, R // 2, R // 2), F32),
        ),
        [SMEM, SMEM, HBM, VMEM],
        [
            halves(PEERS * ROWS2),
            pltpu.VMEM((BLK, BS, BS * BS), BF16),
            pltpu.SemaphoreType.DMA((BLK,)),
        ],
        cost_estimate=pl.CostEstimate(
            flops=2 * BLK * BS * BS * BS * R, bytes_accessed=BLK * BS * BS * BS * 2, transcendentals=0
        ),
    )(block_rows, base, tensor_blocks, got)


def inverse_kernel(state_ref, out_ref):
    half = R // 2
    down = lax.broadcasted_iota(jnp.int32, (half, half), 0)
    along = lax.broadcasted_iota(jnp.int32, (half, half), 1)
    scale, scale_last = state_ref[3, :1], state_ref[4, :1]
    first = state_ref[0]
    middle = dot_high(state_ref[2], first)
    last = finish(eliminate(state_ref[1], down, along))
    out_ref[:half, :half] = first * scale
    out_ref[:half, half:] = jnp.zeros((half, half), F32)
    out_ref[half:, :half] = -dot_high(last, middle) * scale
    out_ref[half:, half:] = last * scale_last


def final_kernel(parts_ref, inverse_ref, out_ref):
    rows = (parts_ref[0] + parts_ref[1]) + (parts_ref[2] + parts_ref[3])
    inverse = inverse_ref[...]
    halfway = dot_high(rows, inverse, ((1,), (1,)))
    out_ref[...] = dot_high(halfway, inverse)


def body(tensor_blocks, block_rows, block_seconds, block_thirds, second_factor, third_factor):
    shape = jax.ShapeDtypeStruct
    exchange = functools.partial(lax.all_to_all, split_axis=0, concat_axis=0, tiled=True)
    x = lax.axis_index("x").astype(jnp.int32).reshape(1)
    wide_at = (lax.axis_index("y") * ZS + lax.axis_index("z")) * CS + lax.axis_index("c")
    base = (wide_at * XS).astype(jnp.int32).reshape(1)

    keep = functools.partial(pltpu.with_memory_space_constraint, memory_space=pltpu.HBM)
    sent = call(
        first_kernel,
        pltpu.HBM((PAIRS, ROWS0, R), BF16),
        [SMEM, HBM, HBM, HBM, HBM],
        [
            halves(PAIRS * ROWS0),
            halves(640),
            pltpu.VMEM((512, R), BF16),
            pltpu.VMEM((128, R), BF16),
            pltpu.VMEM((2, 1, BLK), jnp.int32),
            pltpu.SemaphoreType.DMA((4,)),
        ],
    )(x, *map(keep, (second_factor, third_factor, block_seconds.reshape(1, BLK), block_thirds.reshape(1, BLK))))
    got0 = exchange(sent, ("y", "c"))

    z = lax.axis_index("z").astype(jnp.int32).reshape(1)
    sent, places = call(
        second_kernel,
        (shape((ROWS1, R), BF16), shape((2 * PAIRS, 128), jnp.int32)),
        [SMEM, VMEM],
        [halves(PAIRS * ROWS0), pltpu.VMEM((ROWS1, R), F32)],
    )(z, got0)
    around = [[(z, (z + step) % ZS) for z in range(ZS)] for step in (1, -1)]
    from_low, from_high = [sent], [sent]
    for _ in range(3):
        from_low.append(lax.ppermute(from_low[-1], "z", around[0]))
        from_high.append(lax.ppermute(from_high[-1], "z", around[1]))
    pieces = from_low + from_high[1:] + [lax.ppermute(from_high[-1], "z", around[1])]

    places, _ = lax.optimization_barrier((places, from_high[2]))
    others = [
        lax.ppermute(places, "x", [(n, (n + step) % XS) for n in range(XS)]) for step in (3, 2, 1)
    ]
    places = jnp.stack([*others, places] * 2)
    places = lax.dynamic_slice_in_dim(places, XS - 1 - lax.axis_index("x"), XS, 0)[:, :, :BLK]
    place_two = places[:, :PAIRS].swapaxes(0, 1).reshape(-1)
    place_three = places[:, PAIRS:].swapaxes(0, 1).reshape(-1)

    def one_hot(place, width):
        return (place[:, None] == jnp.arange(width)[None, :]).astype(BF16)

    sent = call(
        third_kernel,
        pltpu.HBM((PEERS, ROWS2, R), BF16),
        [VMEM] * (ZS + 3),
        [
            pltpu.VMEM((PEERS * ROWS2, R), F32),
            pltpu.VMEM((PEERS, ROWS2, R), BF16),
            pltpu.SemaphoreType.DMA((4,)),
        ],
        HBM,
    )(*pieces, one_hot(place_two, 64 * ZS), one_hot(place_three, 32 * ZS), one_hot(place_three + PAIRS, 32 * ZS))
    got2 = exchange(sent, RING)

    summed, state = products(block_rows, base, tensor_blocks, got2)
    parts = exchange(summed.reshape(XS, BS, R), "x")
    inverse = call(
        inverse_kernel,
        shape((R, R), F32),
        [VMEM],
        cost_estimate=pl.CostEstimate(flops=10**9, bytes_accessed=10**6, transcendentals=0),
    )(state)
    return call(final_kernel, shape((BS, R), F32), [VMEM] * 2)(parts, inverse)


def solution(mesh):
    fine = Mesh(mesh.devices.reshape(YS, ZS, CS, XS), ("y", "z", "c", "x"))
    wide, every = ("y", "z", "c"), ("y", "z", "c", "x")
    in_specs = (
        P(every, None, None),
        P(every),
        P(every),
        P(every),
        P(wide, None),
        P(wide, None),
    )
    return jax.shard_map(body, mesh=fine, in_specs=in_specs, out_specs=P(every, None), check_vma=False)
```

```python
import functools
import jax
import jax.numpy as jnp
from jax import lax
from jax.experimental import pallas as pl
from jax.experimental.pallas import tpu as pltpu
from jax.sharding import Mesh, PartitionSpec as P

BS = 64
R = 256
BLK = 24
YS, ZS, CS, XS = 4, 8, 2, 4
PEERS = YS * CS * XS
RING = ("y", "c", "x")
PAIRS = YS * CS
ROWS0 = 48
ROWS1 = 192
ROWS2 = 112
F32 = jnp.float32
BF16 = jnp.bfloat16
VMEM = pl.BlockSpec(memory_space=pltpu.VMEM)
SMEM = pl.BlockSpec(memory_space=pltpu.SMEM)
HBM = pl.BlockSpec(memory_space=pltpu.HBM)
LIMIT = 48 * 1024 * 1024


def call(kernel, out_shape, in_specs, scratch=(), out_spec=VMEM, **kw):
    return pl.pallas_call(
        kernel,
        out_shape=out_shape,
        in_specs=in_specs,
        out_specs=jax.tree.map(lambda _: out_spec, out_shape),
        scratch_shapes=list(scratch),
        compiler_params=pltpu.CompilerParams(vmem_limit_bytes=LIMIT),
        **kw,
    )


def three(value):
    high = value.astype(BF16).astype(F32)
    rest = value - high
    middle = rest.astype(BF16).astype(F32)
    return high, middle, rest - middle


def halves(rows):
    return pltpu.VMEM((2, rows, 128), F32)


def put(wide, start, stride, values):
    for half in range(2):
        wide[half, pl.ds(start, values.shape[0], stride=stride), :] = values[:, 128 * half : 128 * half + 128]


def take(wide, start, stride, count=PEERS):
    return jnp.concatenate([wide[half, pl.ds(start, count, stride=stride), :] for half in range(2)], axis=1)


def fill(wide, values, start=0):
    for half in range(2):
        wide[half, start : start + values.shape[0]] = values[:, 128 * half : 128 * half + 128]


def whole(wide):
    return jnp.concatenate([wide[half] for half in range(2)], axis=1)


def packed_gram(rows):
    gram = lax.dot_general(rows, rows, (((0,), (0,)), ((), ())), preferred_element_type=F32)
    half = R // 2
    down = lax.broadcasted_iota(jnp.int32, (half, half), 0)
    along = lax.broadcasted_iota(jnp.int32, (half, half), 1)
    corner = gram[half:, half:]
    mixed = jnp.where(down >= along, gram[:half, :half], corner)
    diagonal = jnp.sum(jnp.where(down == along, corner, 0.0), axis=1, keepdims=True)
    return jnp.concatenate([mixed, gram[half:, :half]], axis=1), diagonal


def first_kernel(x_ref, second_ref, third_ref, seconds_ref, thirds_ref, out_ref, wide, table, two, few, at, sems):
    x = x_ref[0]
    copies = [
        pltpu.make_async_copy(second_ref, two, sems.at[0]),
        pltpu.make_async_copy(third_ref, few, sems.at[1]),
        pltpu.make_async_copy(seconds_ref, at.at[0], sems.at[2]),
        pltpu.make_async_copy(thirds_ref, at.at[1], sems.at[3]),
    ]
    for copy in copies:
        copy.start()
    for copy in copies:
        copy.wait()

    def mine(start):
        return take(table, start + x, XS, PAIRS)

    fill(table, two[...].astype(F32))
    fill(table, few[...].astype(F32), 512)
    for n in range(20):
        put(wide, 24 + n, ROWS0, mine(32 * n))
    grams = [packed_gram(two[...]), packed_gram(few[...])]
    lane = lax.broadcasted_iota(jnp.int32, (128, R), 1)
    column = jnp.where(lane < 132, grams[0][1], grams[1][1])
    for part, values in enumerate(three(column)):
        fill(table, values, 128 * part)
    lane = lane[:PAIRS]
    seconds = at[0]
    names = (seconds >> 4, seconds & 15, at[1])
    for part in range(3):
        extra = jnp.zeros((PAIRS, R), F32)
        for m in range(4):
            extra = jnp.where((lane == 128 + m) | (lane == 132 + m), mine(128 * part + 32 * m), extra)
        put(wide, 44 + part, ROWS0, extra)
        wide[0, pl.ds(44 + part, PAIRS, stride=ROWS0), :] = jnp.concatenate(
            [jnp.broadcast_to(names[part].astype(F32), (PAIRS, BLK)), jnp.zeros((PAIRS, 128 - BLK), F32)], axis=1
        )
    put(wide, 47, ROWS0, jnp.zeros((PAIRS, R), F32))
    for which in range(2):
        for part, values in enumerate(three(grams[which][0])):
            fill(table, values, 128 * part)
            for m in range(4):
                put(wide, 12 * which + 4 * part + m, ROWS0, mine(128 * part + 32 * m))
    out_ref[...] = whole(wide).astype(BF16).reshape(PAIRS, ROWS0, R)


def second_kernel(z_ref, got_ref, out_ref, places_ref, wide, slab):
    fill(wide, got_ref[...].reshape(PAIRS * ROWS0, R).astype(F32))
    total = got_ref[0].astype(F32)
    for source in range(1, PAIRS):
        total = total + got_ref[source].astype(F32)
    for i in range(2):
        for block in range(8):
            slab[64 * i + 8 * block : 64 * i + 8 * block + 8, :] = take(wide, 24 + 2 * block + i, ROWS0, PAIRS)
    for n in range(4):
        slab[128 + 8 * n : 136 + 8 * n, :] = take(wide, 40 + n, ROWS0, PAIRS)
    chunks = [total[12 * w : 12 * w + 4] + total[12 * w + 4 : 12 * w + 8] + total[12 * w + 8 : 12 * w + 12] for w in range(2)]
    for w in range(2):
        for part, values in enumerate(three(chunks[w])):
            slab[160 + 12 * w + 4 * part : 164 + 12 * w + 4 * part, :] = values
    slab[184:192, :] = jnp.zeros((8, R), F32)
    for part, values in enumerate(three(total[44:45] + total[45:46] + total[46:47])):
        slab[184 + part : 185 + part, :] = values
    out_ref[...] = slab[...].astype(BF16)

    names = [take(wide, 44 + n, ROWS0, PAIRS)[:, :128].astype(jnp.int32) for n in range(3)]
    seconds, thirds = names[0] * 16 + names[1], names[2]

    def source(holder):
        back = (z_ref[0] - (holder >> 1)) & (ZS - 1)
        return ((holder >> 4) << 1) | (holder & 1), jnp.where(back < 4, back, 11 - back)

    pair, plane = source(seconds >> 3)
    place_two = plane * 64 + (seconds & 7) * PAIRS + pair
    pair, plane = source(thirds >> 1)
    place_three = plane * 32 + (thirds & 1) * (2 * PAIRS) + pair
    places_ref[:PAIRS] = place_two
    places_ref[PAIRS:] = place_three


def third_kernel(*refs):
    pieces = refs[:ZS]
    pick_two_ref, pick_left_ref, pick_right_ref, out_ref, wide, narrow, sems = refs[ZS:]

    def table(start, stop):
        return jnp.concatenate([ref[start:stop, :] for ref in pieces], axis=0)

    for i in range(2):
        rows = jnp.dot(pick_two_ref[...], table(64 * i, 64 * i + 64), preferred_element_type=F32)
        for d in range(PEERS):
            wide[d * ROWS2 + BLK * i : d * ROWS2 + BLK * (i + 1), :] = rows[BLK * d : BLK * (d + 1)]
    for i, pick_ref in enumerate((pick_left_ref, pick_right_ref)):
        rows = jnp.dot(pick_ref[...], table(128, 160), preferred_element_type=F32)
        for d in range(PEERS):
            wide[d * ROWS2 + BLK * (2 + i) : d * ROWS2 + BLK * (3 + i), :] = rows[BLK * d : BLK * (d + 1)]
    total = pieces[0][160:, :].astype(F32)
    for ref in pieces[1:]:
        total = total + ref[160:, :].astype(F32)
    gram_two = total[0:4] + total[4:8] + total[8:12]
    gram_three = total[12:16] + total[16:20] + total[20:24]
    normal = three(gram_two * gram_three)
    diagonal = total[24:25] + total[25:26] + total[26:27]
    diagonal = three(diagonal[:, 128:132] * diagonal[:, 132:136])
    for part in range(3):
        wide[96 + 4 * part : 100 + 4 * part, :] = normal[part]
    wide[108:112, :] = jnp.zeros((4, R), F32)
    for part in range(3):
        wide[108 + part : 109 + part, 128:132] = diagonal[part]
    tail = wide[96:112, :]
    for d in range(1, PEERS):
        wide[d * ROWS2 + 96 : d * ROWS2 + 112, :] = tail
    copies = []
    for n in range(4):
        peers = pl.ds(8 * n, 8)
        rows = wide[8 * n * ROWS2 : 8 * (n + 1) * ROWS2, :]
        narrow[peers] = rows.astype(BF16).reshape(8, ROWS2, R)
        copies.append(pltpu.make_async_copy(narrow.at[peers], out_ref.at[peers], sems.at[n]))
        copies[-1].start()
    for copy in copies:
        copy.wait()


def dot_high(a, b, dims=((1,), (0,))):
    return lax.dot_general(
        a, b, (dims, ((), ())), precision=lax.Precision.HIGHEST, preferred_element_type=F32
    )


def reciprocal(value):
    guess = pltpu.reciprocal(value, approx=True)
    return guess * (2.0 - value * guess)


def inverse_root(value):
    guess = lax.rsqrt(value)
    return guess * (1.5 - 0.5 * value * guess * guess)


def eliminate(matrix, down, along):
    size = R // 2
    count = size // 8
    identity = jnp.where(down == along, 1.0, 0.0).astype(F32)
    left = [matrix[8 * g : 8 * g + 8] for g in range(count)]
    right = [identity[8 * g : 8 * g + 8] for g in range(count)]
    sub = lax.broadcasted_iota(jnp.int32, (8, size), 0)

    def row(value, j):
        return jnp.broadcast_to(value[j : j + 1, :], (8, size))

    def columns(g, p):
        return [jnp.broadcast_to(left[g][:, 8 * p + j : 8 * p + j + 1], (8, size)) for j in range(8)]

    for p in range(count):
        pivots = []
        for g in range(p, count):
            spread = columns(g, p)
            new_left, new_right = left[g], right[g]
            for n in range(4):
                j = 2 * n
                if g == p:
                    across = [[row(spread[m], j + i) for m in range(8)] for i in range(2)]
                    a, b, d = across[0][j], across[0][j + 1], across[1][j + 1]
                    scale = reciprocal(a * d - b * b)
                    rows = [row(new_left, j), row(new_left, j + 1), row(new_right, j), row(new_right, j + 1)]
                    pivots.append((across, a, b, d, scale, rows))
                    if n == 3:
                        break
                    first = jnp.where(sub > j + 1, spread[j], 0.0)
                    second = jnp.where(sub > j + 1, spread[j + 1], 0.0)
                else:
                    across, a, b, d, scale, rows = pivots[n]
                    first, second = spread[j], spread[j + 1]
                one = (first * d - second * b) * scale
                two = (second * a - first * b) * scale
                for m in range(j + 2, 8):
                    spread[m] = spread[m] - (one * across[0][m] + two * across[1][m])
                new_left = new_left - (one * rows[0] + two * rows[1])
                new_right = new_right - (one * rows[2] + two * rows[3])
            left[g], right[g] = new_left, new_right
        yield
    left = jnp.concatenate(left, axis=0)
    right = jnp.concatenate(right, axis=0)
    main = jnp.sum(jnp.where(down == along, left, 0.0), axis=1, keepdims=True)
    below = jnp.sum(jnp.where(down == along + 1, left, 0.0), axis=1, keepdims=True)
    above = pltpu.roll(jnp.broadcast_to(main, (size, size)), 1, 0)[:, :1]
    odd = lax.broadcasted_iota(jnp.int32, (size, 1), 0) % 2 == 1
    ratio = jnp.where(odd, below / above, 0.0)
    return (right - ratio * pltpu.roll(right, 1, 0)) * inverse_root(main - ratio * below)


def finish(steps):
    while True:
        try:
            next(steps)
        except StopIteration as stop:
            return stop.value


def scaled_normal(wide, down, along):
    half = R // 2
    packed, diagonal = [], []
    for m in range(4):
        rows = [take(wide, 96 + 4 * part + m, ROWS2) for part in range(3)]
        packed.append(rows[0] + rows[1] + rows[2])
        rows = [take(wide, 108 + part, ROWS2) for part in range(3)]
        diagonal.append((rows[0] + rows[1] + rows[2])[:, 128 + m : 129 + m])
    packed = jnp.concatenate(packed, axis=0)
    diagonal = jnp.concatenate(diagonal, axis=0)
    mixed = packed[:, :half]
    flipped = mixed.T
    upper = jnp.where(down >= along, mixed, flipped)
    corner = jnp.where(down == along, diagonal, jnp.where(down < along, mixed, flipped))
    scales = [
        [inverse_root(jnp.sum(jnp.where(down == along, part, 0.0), axis=axis, keepdims=True)) for axis in (1, 0)]
        for part in (upper, corner)
    ]
    upper = upper * scales[0][0] * scales[0][1]
    below = packed[:, half:] * scales[1][0] * scales[0][1]
    corner = corner * scales[1][0] * scales[1][1]
    return upper, below, corner, scales[0][1], scales[1][1]


def product_kernel(rows_ref, base_ref, x_ref, tensor_ref, got_ref, *refs):
    out_refs, (state_ref, out_ref, wide, blocks, sems) = refs[:XS], refs[XS:]

    def fetch(t):
        return pltpu.make_async_copy(tensor_ref.at[t], blocks.at[t], sems.at[t])

    for t in range(BLK):
        fetch(t).start()
    fill(wide, got_ref[...].reshape(PEERS * ROWS2, R).astype(F32))
    out_ref[...] = jnp.zeros_like(out_ref)
    half = R // 2
    down = lax.broadcasted_iota(jnp.int32, (half, half), 0)
    along = lax.broadcasted_iota(jnp.int32, (half, half), 1)
    upper, below, corner, scale, scale_last = scaled_normal(wide, down, along)
    steps = eliminate(upper, down, along)

    def one_block(t):
        left = [take(wide, BLK * i + t, ROWS2) for i in range(2)]
        right = jnp.concatenate([take(wide, BLK * (2 + i) + t, ROWS2) for i in range(2)], axis=0)
        right = right.astype(BF16)

        total = jnp.zeros((BS, R), F32)
        for q in range(BS // 4):
            parts = []
            for b in range(4 * q, 4 * q + 4):
                row = left[b // 32][b % 32 : b % 32 + 1, :]
                row = jnp.broadcast_to(row, (16, R)).astype(BF16)
                parts.append(jnp.concatenate([row] * 4, axis=0) * right)
            total = total + jnp.dot(
                blocks[t, :, 256 * q : 256 * q + 256],
                jnp.concatenate(parts, axis=0),
                preferred_element_type=F32,
            )
        place = pl.multiple_of(((rows_ref[t] - base_ref[0] - x_ref[0]) & (XS - 1)) * BS, BS)
        out_ref[pl.ds(place, BS), :] += total

    taken = 0
    for t in range(BLK):
        for later in range(t, {0: 2, 2: 8, 8: BLK}.get(t, t)):
            fetch(later).wait()
        one_block(t)
        while taken < min(half // 8, (t + 1) * half // 8 // (BLK - 4)):
            next(steps)
            taken += 1
    for n in range(XS):
        out_refs[n][...] = out_ref[BS * n : BS * (n + 1), :]
    first = finish(steps)
    lower = dot_high(below, first, ((1,), (1,)))
    state_ref[0] = first
    state_ref[1] = corner - dot_high(lower, lower, ((1,), (1,)))
    state_ref[2] = lower
    state_ref[3] = jnp.broadcast_to(scale, (half, half))
    state_ref[4] = jnp.broadcast_to(scale_last, (half, half))


def products(block_rows, base, x, tensor_blocks, got):
    return call(
        product_kernel,
        (
            *[jax.ShapeDtypeStruct((BS, R), F32)] * XS,
            jax.ShapeDtypeStruct((5, R // 2, R // 2), F32),
        ),
        [SMEM, SMEM, SMEM, HBM, VMEM],
        [
            pltpu.VMEM((XS * BS, R), F32),
            halves(PEERS * ROWS2),
            pltpu.VMEM((BLK, BS, BS * BS), BF16),
            pltpu.SemaphoreType.DMA((BLK,)),
        ],
        cost_estimate=pl.CostEstimate(
            flops=2 * BLK * BS * BS * BS * R, bytes_accessed=BLK * BS * BS * BS * 2, transcendentals=0
        ),
    )(block_rows, base, x, tensor_blocks, got)


def inverse_kernel(state_ref, out_ref):
    half = R // 2
    down = lax.broadcasted_iota(jnp.int32, (half, half), 0)
    along = lax.broadcasted_iota(jnp.int32, (half, half), 1)
    scale, scale_last = state_ref[3, :1], state_ref[4, :1]
    first = state_ref[0]
    middle = dot_high(state_ref[2], first)
    last = finish(eliminate(state_ref[1], down, along))
    out_ref[:half, :half] = first * scale
    out_ref[:half, half:] = jnp.zeros((half, half), F32)
    out_ref[half:, :half] = -dot_high(last, middle) * scale
    out_ref[half:, half:] = last * scale_last


def final_kernel(*refs):
    parts, (inverse_ref, out_ref) = [ref[...] for ref in refs[:XS]], refs[XS:]
    rows = (parts[0] + parts[1]) + (parts[2] + parts[3])
    inverse = inverse_ref[...]
    halfway = dot_high(rows, inverse, ((1,), (1,)))
    out_ref[...] = dot_high(halfway, inverse)


def body(tensor_blocks, block_rows, block_seconds, block_thirds, second_factor, third_factor):
    shape = jax.ShapeDtypeStruct
    exchange = functools.partial(lax.all_to_all, split_axis=0, concat_axis=0, tiled=True)
    x = lax.axis_index("x").astype(jnp.int32).reshape(1)
    wide_at = (lax.axis_index("y") * ZS + lax.axis_index("z")) * CS + lax.axis_index("c")
    base = (wide_at * XS).astype(jnp.int32).reshape(1)

    keep = functools.partial(pltpu.with_memory_space_constraint, memory_space=pltpu.HBM)
    sent = call(
        first_kernel,
        pltpu.HBM((PAIRS, ROWS0, R), BF16),
        [SMEM, HBM, HBM, HBM, HBM],
        [
            halves(PAIRS * ROWS0),
            halves(640),
            pltpu.VMEM((512, R), BF16),
            pltpu.VMEM((128, R), BF16),
            pltpu.VMEM((2, 1, BLK), jnp.int32),
            pltpu.SemaphoreType.DMA((4,)),
        ],
    )(x, *map(keep, (second_factor, third_factor, block_seconds.reshape(1, BLK), block_thirds.reshape(1, BLK))))
    got0 = exchange(sent, ("y", "c"))

    z = lax.axis_index("z").astype(jnp.int32).reshape(1)
    sent, places = call(
        second_kernel,
        (shape((ROWS1, R), BF16), shape((2 * PAIRS, 128), jnp.int32)),
        [SMEM, VMEM],
        [halves(PAIRS * ROWS0), pltpu.VMEM((ROWS1, R), F32)],
    )(z, got0)
    around = [[(z, (z + step) % ZS) for z in range(ZS)] for step in (1, -1)]
    from_low, from_high = [sent], [sent]
    for _ in range(3):
        from_low.append(lax.ppermute(from_low[-1], "z", around[0]))
        from_high.append(lax.ppermute(from_high[-1], "z", around[1]))
    pieces = from_low + from_high[1:] + [lax.ppermute(from_high[-1], "z", around[1])]

    places, _ = lax.optimization_barrier((places, from_high[2]))
    others = [
        lax.ppermute(places, "x", [(n, (n + step) % XS) for n in range(XS)]) for step in (3, 2, 1)
    ]
    places = jnp.stack([*others, places] * 2)
    places = lax.dynamic_slice_in_dim(places, XS - 1 - lax.axis_index("x"), XS, 0)[:, :, :BLK]
    place_two = places[:, :PAIRS].swapaxes(0, 1).reshape(-1)
    place_three = places[:, PAIRS:].swapaxes(0, 1).reshape(-1)

    def one_hot(place, width):
        return (place[:, None] == jnp.arange(width)[None, :]).astype(BF16)

    sent = call(
        third_kernel,
        pltpu.HBM((PEERS, ROWS2, R), BF16),
        [VMEM] * (ZS + 3),
        [
            pltpu.VMEM((PEERS * ROWS2, R), F32),
            pltpu.VMEM((PEERS, ROWS2, R), BF16),
            pltpu.SemaphoreType.DMA((4,)),
        ],
        HBM,
    )(*pieces, one_hot(place_two, 64 * ZS), one_hot(place_three, 32 * ZS), one_hot(place_three + PAIRS, 32 * ZS))
    got2 = exchange(sent, RING)

    *summed, state = products(block_rows, base, x, tensor_blocks, got2)
    parts = [summed[0]] + [
        lax.ppermute(summed[step], "x", [(n, (n + step) % XS) for n in range(XS)]) for step in (1, 2, 3)
    ]
    inverse = call(
        inverse_kernel,
        shape((R, R), F32),
        [VMEM],
        cost_estimate=pl.CostEstimate(flops=10**9, bytes_accessed=10**6, transcendentals=0),
    )(state)
    return call(final_kernel, shape((BS, R), F32), [VMEM] * (XS + 1))(*parts, inverse)


def solution(mesh):
    fine = Mesh(mesh.devices.reshape(YS, ZS, CS, XS), ("y", "z", "c", "x"))
    wide, every = ("y", "z", "c"), ("y", "z", "c", "x")
    in_specs = (
        P(every, None, None),
        P(every),
        P(every),
        P(every),
        P(wide, None),
        P(wide, None),
    )
    return jax.shard_map(body, mesh=fine, in_specs=in_specs, out_specs=P(every, None), check_vma=False)
```
